512 devices in a mesh: bx: 32 (over x, y, core), by: 16 (over z).
Axes of the slice: x: 4, y: 4, z: 16, core: 2. Of those that a mesh axis runs over, the one named last changes fastest.
Arguments:
- volume: bfloat16 [512, 512, 2048], P('bx', 'by'), may hold values from 0 to 2
- view_side: int32 [512], P('by'), may hold values from 0 to 1
Outputs:
- image: float32 [4, 512, 2048], P(None, 'by', 'bx')
The draws below stay inside these ranges and needn't reach their ends.
All inputs are finite; a program needn't handle non-finite values.
Results may differ from the reference program's by a relative error of at most 0.0003.
Values may be sent and summed in bfloat16 or wider, within the bound.
No kernel may reach another device: no remote copies, remote signals or barrier semaphores. Data moves between devices by JAX's collectives and lax.ppermute only.
A program may use at most 64 MiB of HBM per device.

```python
import jax
import jax.numpy as jnp
from jax import lax

CY = 32
NX = 512
NY = 512
NZ = 2048


def set_ends(entries, own_key, smallest, top_value):
    longest = entries.shape.index(max(entries.shape))
    spots = []
    for shift in (0, 1):
        where = [jax.random.randint(jax.random.fold_in(own_key, axis), (), 0, length) for axis, length in enumerate(entries.shape)]
        where[longest] = (where[longest] + shift) % entries.shape[longest]
        spots.append(tuple(where))
    return entries.at[spots[0]].set(smallest).at[spots[1]].set(top_value)


def level_of(key, extent, split, least, high):
    def one(position, shards_of):
        draws = jax.random.uniform(jax.random.fold_in(jax.random.fold_in(key, 6), position), (shards_of,), jnp.float32, least / len(split), high / len(split))
        return jnp.repeat(jnp.exp(draws), extent[position] // shards_of).reshape((-1,) + (1,) * (len(extent) - position - 1))

    loudness = one(*split[0])
    for cut in split[1:]:
        loudness = loudness * one(*cut)
    return loudness


def setup_inputs(seed: int = 0) -> dict:
    keys = jax.random.split(jax.random.key(seed), 3)
    return {
        "volume": jnp.clip(2.0 * jax.random.uniform(keys[0], (NX, NY, NZ), jnp.float32) ** level_of(keys[0], (NX, NY, NZ), ((0, 32), (1, 16)), -0.2, 0.2), 0.0, 2.0).astype(jnp.bfloat16),
        "view_side": set_ends(jax.random.randint(keys[1], (NY,), 0, 2), jax.random.fold_in(keys[1], 1), 0, 1).astype(jnp.int32),
    }


def shade_block(stencil, ray_length):
    stress = stencil[1:-1, 1:-1, 1:-1]
    grad_x = 0.5 * (stencil[2:, 1:-1, 1:-1] - stencil[:-2, 1:-1, 1:-1])
    grad_y = 0.5 * (stencil[1:-1, 2:, 1:-1] - stencil[1:-1, :-2, 1:-1])
    grad_z = 0.5 * (stencil[1:-1, 1:-1, 2:] - stencil[1:-1, 1:-1, :-2])
    grad_sq = grad_x * grad_x + grad_y * grad_y + grad_z * grad_z
    facing = 0.48 * grad_x + 0.6 * grad_y + 0.64 * grad_z
    shading = 0.3 + 0.7 * facing * facing / (grad_sq + 1.0)
    contour = grad_sq / (grad_sq + 0.25)
    density = jnp.clip((stress - 0.4) / 1.2, 0.0, 1.0)
    opacity = 1.0 - jnp.exp(-3.0 * density * (0.25 + contour) / ray_length)
    weight = opacity * shading
    red_part = jnp.clip(stress - 0.8, 0.0, 1.0)
    green_part = 1.0 - jnp.abs(stress - 1.0)
    blue_part = jnp.clip(1.2 - stress, 0.0, 1.0)
    return jnp.stack([weight * red_part, weight * green_part, weight * blue_part, 1.0 - opacity])


def reference(volume, view_side):
    ray_length = volume.shape[0]
    padded = jnp.pad(volume, 1)

    def render_block(block):
        start = (block * CY).astype(jnp.int32)
        stencil = lax.dynamic_slice(padded, (jnp.int32(0), start, jnp.int32(0)), (ray_length + 2, CY + 2, NZ + 2)).astype(jnp.float32)
        samples = shade_block(stencil, ray_length)
        row_sides = lax.dynamic_slice(view_side, (start,), (CY,))
        reversed_rows = (row_sides == 1)[None, None, :, None]
        samples = jnp.where(reversed_rows, jnp.flip(samples, 1), samples)
        samples = jnp.moveaxis(samples, 1, 0)

        def accumulate(carried, sample):
            color, passing = carried
            color = color + passing[None] * sample[:3]
            passing = passing * sample[3]
            return (color, passing), None

        start_state = (jnp.zeros((3, CY, NZ), jnp.float32), jnp.ones((CY, NZ), jnp.float32))
        (color, passing), unused = lax.scan(accumulate, start_state, samples)
        return jnp.concatenate([color, (1.0 - passing)[None]], 0)

    blocks = lax.map(render_block, jnp.arange(NY // CY, dtype=jnp.int32))
    return jnp.transpose(blocks, (1, 0, 2, 3)).reshape(4, NY, NZ)
```

```python
import functools
import math

import jax
import jax.numpy as jnp
from jax import lax
from jax.experimental import pallas as pl
from jax.experimental.pallas import tpu as pltpu
from jax.sharding import PartitionSpec as P

F32 = jnp.float32
LANES = 128
TILES = 4
LOG2E = 1.0 / math.log(2.0)
FLOOR = -27.0
STEPS = 2621.0


def recip(x):
    return pl.reciprocal(x, approx=True)


def lane_tile(start):
    return pl.ds(pl.multiple_of(start, LANES), LANES)


def encode(value):
    level = jnp.log2(jnp.maximum(value, 2.0**FLOOR)) * STEPS + (0.5 - FLOOR * STEPS)
    return jnp.minimum(level, 65535.0).astype(jnp.int32) - 32768


def decode(code):
    code = code.astype(jnp.int32)
    value = jnp.exp2(code.astype(F32) * (1.0 / STEPS) + (32768.0 / STEPS + FLOOR))
    return jnp.where(code == -32768, 0.0, value)


def render_kernel(ray_length, vol, before, after, above, below, sign, codes, field, image):
    layers, rows, depth = vol.shape
    width = LANES * TILES
    chunks = depth // width
    scale = 3.0 / 1.2 / ray_length * LOG2E
    tone = math.sqrt(0.7)
    lane = lax.broadcasted_iota(jnp.int32, (8, LANES), 1)

    def chunk(c, carry):
        base = c * width

        def widen(l, carry):
            for t in range(TILES):
                field[l + 1, t + 1, pl.ds(8, rows), :] = vol[l, :, lane_tile(base + LANES * t)].astype(F32)
            left = lane_tile(jnp.maximum(base - LANES, 0))
            right = lane_tile(jnp.minimum(base + width, depth - LANES))
            field[l + 1, 0, pl.ds(8, rows), :] = jnp.where(c == 0, 0.0, vol[l, :, left].astype(F32))
            field[l + 1, TILES + 1, pl.ds(8, rows), :] = jnp.where(c == chunks - 1, 0.0, vol[l, :, right].astype(F32))
            return carry

        lax.fori_loop(0, layers, widen, 0, unroll=4)
        for t in range(TILES):
            here = lane_tile(base + LANES * t)
            field[pl.ds(1, layers), t + 1, 7, :] = above[:, here].astype(F32)
            field[pl.ds(1, layers), t + 1, rows + 8, :] = below[:, here].astype(F32)
            field[0, t + 1, pl.ds(8, rows), :] = before[0, :, here].astype(F32)
            field[layers + 1, t + 1, pl.ds(8, rows), :] = after[0, :, here].astype(F32)

        def row_block(r, carry):
            r8 = pl.multiple_of(8 * r, 8)
            side = sign[pl.ds(r8, 8), :]
            most = side * (1.25 * scale)
            part = side * scale
            path = [jnp.zeros((8, LANES), F32) for _ in range(TILES)]
            reach = [jnp.ones((8, LANES), F32) for _ in range(TILES)]
            color = [[jnp.zeros((8, LANES), F32) for _ in range(TILES)] for _ in range(3)]
            for l in range(layers):
                mid = [field[l + 1, t, pl.ds(r8 + 8, 8), :] for t in range(TILES + 2)]
                from_left = [pltpu.roll(v, 1, 1) for v in mid[:-1]]
                from_right = [pltpu.roll(v, LANES - 1, 1) for v in mid[1:]]
                for t in range(TILES):
                    v = mid[t + 1]
                    gz = jnp.where(lane == LANES - 1, from_right[t + 1], from_right[t]) - jnp.where(
                        lane == 0, from_left[t], from_left[t + 1]
                    )
                    gy = field[l + 1, t + 1, pl.ds(r8 + 9, 8), :] - field[l + 1, t + 1, pl.ds(r8 + 7, 8), :]
                    gx = field[l + 2, t + 1, pl.ds(r8 + 8, 8), :] - field[l, t + 1, pl.ds(r8 + 8, 8), :]
                    square = gx * gx + gy * gy + gz * gz
                    facing = (0.48 * tone) * gx + (0.6 * tone) * gy + (0.64 * tone) * gz
                    shading = 0.3 + facing * facing * recip(square + 4.0)
                    density = jnp.clip(v - 0.4, 0.0, 1.2)
                    path[t] = path[t] + density * (most - part * recip(square + 1.0))
                    next_reach = jnp.exp2(path[t])
                    weight = (next_reach - reach[t]) * shading
                    reach[t] = next_reach
                    color[0][t] = color[0][t] + weight * jnp.clip(v - 0.8, 0.0, 1.0)
                    color[1][t] = color[1][t] + weight * jnp.minimum(v, 2.0 - v)
                    color[2][t] = color[2][t] + weight * jnp.clip(1.2 - v, 0.0, 1.0)
            for t in range(TILES):
                here = lane_tile(base + LANES * t)
                factor = jnp.where(side > 0, jnp.exp2(-path[t]), -1.0)
                for k in range(3):
                    image[k, pl.ds(r8, 8), here] = color[k][t] * factor
                image[3, pl.ds(r8, 8), here] = path[t] * side
            return carry

        lax.fori_loop(0, rows // 8, row_block, 0)
        return carry

    lax.fori_loop(0, chunks, chunk, 0)
    half = rows // 2
    low = lax.broadcasted_iota(jnp.int32, (half, LANES), 1) < LANES // 2

    def pack(z, carry):
        here = lane_tile(LANES * z)
        for k in range(4):
            top = encode(image[k, pl.ds(0, half), here])
            bottom = encode(image[k, pl.ds(half, half), here])
            codes[2 * z, k] = jnp.where(low, top, pltpu.roll(bottom, LANES // 2, 1)).astype(jnp.int16)
            codes[2 * z + 1, k] = jnp.where(low, pltpu.roll(top, LANES // 2, 1), bottom).astype(jnp.int16)
        return carry

    lax.fori_loop(0, depth // LANES, pack, 0, unroll=2)


def fold_kernel(codes, sign, out):
    bricks, _, half, _ = codes.shape
    side = sign[...]
    backward = side > 0
    path = jnp.zeros((half, LANES), F32)
    color = [jnp.zeros((half, LANES), F32) for _ in range(3)]
    for k in range(bricks):
        farther = path + decode(codes[k, 3])
        reach = jnp.exp2(side * jnp.where(backward, farther, path))
        path = farther
        for q in range(3):
            color[q] = color[q] + reach * decode(codes[k, q])
    passing = jnp.exp2(-path)
    factor = jnp.where(backward, passing, 1.0)
    parts = [c * factor for c in color] + [1.0 - passing]
    for q in range(4):
        out[q, pl.ds(0, half), :] = parts[q][:, : LANES // 2]
        out[q, pl.ds(half, half), :] = parts[q][:, LANES // 2 :]


def body(volume, view_side):
    layers, rows, depth = volume.shape
    size_x, size_y = lax.axis_size("bx"), lax.axis_size("by")
    up_x = [(i, i + 1) for i in range(size_x - 1)]
    up_y = [(i, i + 1) for i in range(size_y - 1)]
    down_x = [(j, i) for i, j in up_x]
    down_y = [(j, i) for i, j in up_y]
    above = lax.ppermute(volume[:, rows - 1, :], "by", up_y)
    below = lax.ppermute(volume[:, 0, :], "by", down_y)
    before = lax.ppermute(volume[layers - 1 :], "bx", up_x)
    after = lax.ppermute(volume[:1], "bx", down_x)
    side = jnp.where(view_side == 1, 1.0, -1.0).astype(F32)
    sign = jnp.broadcast_to(side[:, None], (rows, LANES))
    half = rows // 2
    both = jnp.concatenate([sign[:half, : LANES // 2], sign[half:, : LANES // 2]], 1)
    in_vmem = pl.BlockSpec(memory_space=pltpu.VMEM)
    codes = pl.pallas_call(
        functools.partial(render_kernel, layers * size_x),
        out_shape=jax.ShapeDtypeStruct((size_x, 4, half, LANES), jnp.int16),
        in_specs=[in_vmem] * 6,
        out_specs=in_vmem,
        scratch_shapes=[
            pltpu.VMEM((layers + 2, TILES + 2, rows + 16, LANES), F32),
            pltpu.VMEM((4, rows, depth), F32),
        ],
        compiler_params=pltpu.CompilerParams(vmem_limit_bytes=40 << 20),
        name="render",
    )(volume, before, after, above, below, sign)
    codes = lax.all_to_all(codes, "bx", split_axis=0, concat_axis=0, tiled=True)
    return pl.pallas_call(
        fold_kernel,
        out_shape=jax.ShapeDtypeStruct((4, rows, depth // size_x), F32),
        in_specs=[in_vmem] * 2,
        out_specs=in_vmem,
        compiler_params=pltpu.CompilerParams(vmem_limit_bytes=32 << 20),
        name="fold",
    )(codes, both)


def solution(mesh):
    placed = (P("bx", "by", None), P("by"))
    return jax.shard_map(body, mesh=mesh, in_specs=placed, out_specs=P(None, "by", "bx"), check_vma=False)
```

```python
import functools
import math

import jax
import jax.numpy as jnp
from jax import lax
from jax.experimental import pallas as pl
from jax.experimental.pallas import tpu as pltpu
from jax.sharding import PartitionSpec as P

F32 = jnp.float32
BF16 = jnp.bfloat16
LANES = 128
TILES = 4
LOG2E = 1.0 / math.log(2.0)
FLOOR = -27.0
STEPS = 2621.0
TONE = 0.7 * 0.48 * 0.48


def recip(x):
    return pl.reciprocal(x, approx=True)


def lane_tile(start):
    return pl.ds(pl.multiple_of(start, LANES), LANES)


def encode(value):
    level = jnp.log2(jnp.maximum(value, 2.0**FLOOR)) * STEPS + (0.5 - FLOOR * STEPS)
    return jnp.minimum(level, 65535.0).astype(jnp.int32) - 32768


def decode(code):
    code = code.astype(jnp.int32)
    value = jnp.exp2(code.astype(F32) * (1.0 / STEPS) + (32768.0 / STEPS + FLOOR))
    return jnp.where(code == -32768, 0.0, value)


def side_column(view):
    rows = view.shape[1]
    spread = jnp.broadcast_to(view[...].astype(F32), (rows, rows))
    down = lax.broadcasted_iota(jnp.int32, (rows, rows), 0)
    along = lax.broadcasted_iota(jnp.int32, (rows, rows), 1)
    picked = jnp.sum(jnp.where(down == along, spread, 0.0), axis=1, keepdims=True)
    return jnp.where(picked > 0.5, 1.0, -1.0)


def edge_kernel(vol, first_row, last_row, first_layer, last_layer):
    layers, rows, depth = vol.shape

    def tile(z, carry):
        here = lane_tile(LANES * z)
        first_row[:, here] = jnp.concatenate([vol[l, :, here].astype(F32)[:1] for l in range(layers)], 0).astype(BF16)
        last_row[:, here] = jnp.concatenate([vol[l, :, here].astype(F32)[rows - 1 :] for l in range(layers)], 0).astype(BF16)
        first_layer[:, here] = vol[0, :, here]
        last_layer[:, here] = vol[layers - 1, :, here]
        return carry

    lax.fori_loop(0, depth // LANES, tile, 0, unroll=2)


class Sweep:
    def __init__(self, vol, fields, ray_length, halo=None):
        self.vol, self.fields, self.halo = vol, fields, halo
        self.layers, self.rows, self.depth = vol.shape
        self.width = LANES * TILES
        self.chunks = self.depth // self.width
        self.scale = 3.0 / 1.2 / ray_length * LOG2E
        self.lane = lax.broadcasted_iota(jnp.int32, (8, LANES), 1)

    def widen_layer(self, field, c, l):
        base = c * self.width
        inside = pl.ds(8, self.rows)
        for t in range(TILES):
            field[l + 1, t + 1, inside, :] = self.vol[l, :, lane_tile(base + LANES * t)].astype(F32)
        left = lane_tile(jnp.maximum(base - LANES, 0))
        right = lane_tile(jnp.minimum(base + self.width, self.depth - LANES))
        field[l + 1, 0, inside, :] = jnp.where(c == 0, 0.0, self.vol[l, :, left].astype(F32))
        field[l + 1, TILES + 1, inside, :] = jnp.where(c == self.chunks - 1, 0.0, self.vol[l, :, right].astype(F32))

    def widen_halo(self, field, c, t):
        before, after, above, below = self.halo
        here = lane_tile(c * self.width + LANES * t)
        inside = pl.ds(8, self.rows)
        field[0, t + 1, inside, :] = before[:, here].astype(F32)
        field[self.layers + 1, t + 1, inside, :] = after[:, here].astype(F32)
        field[pl.ds(1, self.layers), t + 1, 7, :] = above[:, here].astype(F32)
        field[pl.ds(1, self.layers), t + 1, self.rows + 8, :] = below[:, here].astype(F32)

    def quarter(self, field, c, p):
        each = self.layers // 4
        tasks = [functools.partial(self.widen_layer, field, c, each * p + k) for k in range(each)]
        if self.halo is not None:
            tasks.append(functools.partial(self.widen_halo, field, c, p))
        return tasks

    def fresh(self):
        return dict(
            path=[jnp.zeros((8, LANES), F32) for _ in range(TILES)],
            reach=[jnp.ones((8, LANES), F32) for _ in range(TILES)],
            color=[[jnp.zeros((8, LANES), F32) for _ in range(TILES)] for _ in range(4)],
        )

    def layer(self, field, r8, side, state, l):
        lane = self.lane
        most, part = side * (1.25 * self.scale), side * self.scale
        path, reach, color = state["path"], state["reach"], state["color"]
        mid = [field[l + 1, t, pl.ds(r8 + 8, 8), :] for t in range(TILES + 2)]
        from_left = [pltpu.roll(v, 1, 1) for v in mid[:-1]]
        from_right = [pltpu.roll(v, LANES - 1, 1) for v in mid[1:]]
        for t in range(TILES):
            v = mid[t + 1]
            gz = jnp.where(lane == LANES - 1, from_right[t + 1], from_right[t]) - jnp.where(
                lane == 0, from_left[t], from_left[t + 1]
            )
            gy = field[l + 1, t + 1, pl.ds(r8 + 9, 8), :] - field[l + 1, t + 1, pl.ds(r8 + 7, 8), :]
            gx = field[l + 2, t + 1, pl.ds(r8 + 8, 8), :] - field[l, t + 1, pl.ds(r8 + 8, 8), :]
            square = gx * gx + gy * gy + gz * gz
            facing = gx + (0.6 / 0.48) * gy + (0.64 / 0.48) * gz
            shading = 0.3 / TONE + facing * facing * recip(square + 4.0)
            density = jnp.clip(v - 0.4, 0.0, 1.2)
            path[t] = path[t] + density * (most - part * recip(square + 1.0))
            next_reach = jnp.exp2(path[t])
            weight = (next_reach - reach[t]) * shading
            reach[t] = next_reach
            color[0][t] = color[0][t] + weight * jnp.clip(v, 0.8, 1.8)
            color[1][t] = color[1][t] + weight * jnp.minimum(v, 2.0 - v)
            color[2][t] = color[2][t] + weight * jnp.clip(v, 0.2, 1.2)
            color[3][t] = color[3][t] + weight

    def run(self, work):
        even, odd = self.fields
        for p in range(4):
            for task in self.quarter(even, 0, p):
                task()

        def pair(k, carry):
            for now, later, c in ((even, odd, 2 * k), (odd, even, 2 * k + 1)):
                following = jnp.minimum(c + 1, self.chunks - 1)

                def half(q, carry, now=now, later=later, c=c, following=following):
                    tasks = self.quarter(later, following, 2 * q) + self.quarter(later, following, 2 * q + 1)
                    work(now, c, q, tasks)
                    return carry

                lax.fori_loop(0, 2, half, 0)
            return carry

        lax.fori_loop(0, self.chunks // 2, pair, 0)


def inner_kernel(ray_length, vol, view, part, even, odd, sign):
    sweep = Sweep(vol, (even, odd), ray_length)
    rows = sweep.rows
    sign[...] = jnp.broadcast_to(side_column(view), (rows, LANES))

    def work(field, c, q, tasks):
        r8 = pl.multiple_of(8 + 8 * q, 8)
        side = sign[pl.ds(r8, 8), :]
        state = sweep.fresh()
        for l in range(1, sweep.layers - 1):
            sweep.layer(field, r8, side, state, l)
            if tasks:
                tasks.pop(0)()
        while tasks:
            tasks.pop(0)()
        for t in range(TILES):
            here = lane_tile(c * sweep.width + LANES * t)
            for k, kind in enumerate([state["path"]] + state["color"]):
                part[k, pl.ds(pl.multiple_of(8 * q, 8), 8), here] = kind[t]

    sweep.run(work)


def outer_kernel(ray_length, vol, before, after, above, below, view, part, codes, even, odd, sign, image):
    sweep = Sweep(vol, (even, odd), ray_length, (before, after, above, below))
    layers, rows, depth = vol.shape
    sign[...] = jnp.broadcast_to(side_column(view), (rows, LANES))

    def finish(c, r8, side, state):
        for t in range(TILES):
            here = lane_tile(c * sweep.width + LANES * t)
            path = state["path"][t]
            red, green, blue, total = (kind[t] for kind in state["color"])
            factor = jnp.where(side > 0, jnp.exp2(-path), -1.0) * TONE
            image[0, pl.ds(r8, 8), here] = (red - 0.8 * total) * factor
            image[1, pl.ds(r8, 8), here] = green * factor
            image[2, pl.ds(r8, 8), here] = (1.2 * total - blue) * factor
            image[3, pl.ds(r8, 8), here] = path * side

    def work(field, c, q, tasks):
        r8 = pl.multiple_of(24 * q, 8)
        side = sign[pl.ds(r8, 8), :]
        state = sweep.fresh()
        for l in range(layers):
            sweep.layer(field, r8, side, state, l)
            if tasks:
                tasks.pop(0)()
        while tasks:
            tasks.pop(0)()
        finish(c, r8, side, state)
        r8 = pl.multiple_of(8 + 8 * q, 8)
        side = sign[pl.ds(r8, 8), :]
        state = sweep.fresh()
        sweep.layer(field, r8, side, state, 0)
        for t in range(TILES):
            here = lane_tile(c * sweep.width + LANES * t)
            block = [part[k, pl.ds(pl.multiple_of(8 * q, 8), 8), here] for k in range(5)]
            for k in range(4):
                state["color"][k][t] = state["color"][k][t] + state["reach"][t] * block[k + 1]
            state["path"][t] = state["path"][t] + block[0]
            state["reach"][t] = jnp.exp2(state["path"][t])
        sweep.layer(field, r8, side, state, layers - 1)
        finish(c, r8, side, state)

    sweep.run(work)
    half = rows // 2
    low = lax.broadcasted_iota(jnp.int32, (half, LANES), 1) < LANES // 2

    def pack(z, carry):
        here = lane_tile(LANES * z)
        for k in range(4):
            top = encode(image[k, pl.ds(0, half), here])
            bottom = encode(image[k, pl.ds(half, half), here])
            codes[2 * z, k] = jnp.where(low, top, pltpu.roll(bottom, LANES // 2, 1)).astype(jnp.int16)
            codes[2 * z + 1, k] = jnp.where(low, pltpu.roll(top, LANES // 2, 1), bottom).astype(jnp.int16)
        return carry

    lax.fori_loop(0, depth // LANES, pack, 0, unroll=2)


def fold_kernel(codes, view, out):
    bricks, _, half, _ = codes.shape
    column = side_column(view)
    low = lax.broadcasted_iota(jnp.int32, (half, LANES), 1) < LANES // 2
    side = jnp.where(low, column[:half], column[half:])
    backward = side > 0
    path = jnp.zeros((half, LANES), F32)
    color = [jnp.zeros((half, LANES), F32) for _ in range(3)]
    for k in range(bricks):
        farther = path + decode(codes[k, 3])
        reach = jnp.exp2(side * jnp.where(backward, farther, path))
        path = farther
        for q in range(3):
            color[q] = color[q] + reach * decode(codes[k, q])
    passing = jnp.exp2(-path)
    factor = jnp.where(backward, passing, 1.0)
    parts = [c * factor for c in color] + [1.0 - passing]
    for q in range(4):
        out[q, pl.ds(0, half), :] = parts[q][:, : LANES // 2]
        out[q, pl.ds(half, half), :] = parts[q][:, LANES // 2 :]


def body(volume, view_side):
    layers, rows, depth = volume.shape
    size_x, size_y = lax.axis_size("bx"), lax.axis_size("by")
    up_x = [(i, i + 1) for i in range(size_x - 1)]
    up_y = [(i, i + 1) for i in range(size_y - 1)]
    down_x = [(j, i) for i, j in up_x]
    down_y = [(j, i) for i, j in up_y]
    view = view_side[None, :]
    half = rows // 2
    in_vmem = pl.BlockSpec(memory_space=pltpu.VMEM)
    shape = jax.ShapeDtypeStruct

    def call(kernel, operands, out_shape, scratch, name, cost=None, limit=24):
        return pl.pallas_call(
            kernel,
            out_shape=out_shape,
            in_specs=[in_vmem] * len(operands),
            out_specs=jax.tree.map(lambda _: in_vmem, out_shape),
            scratch_shapes=scratch,
            compiler_params=pltpu.CompilerParams(vmem_limit_bytes=limit << 20),
            cost_estimate=cost,
            name=name,
        )(*operands)

    field = pltpu.VMEM((layers + 2, TILES + 2, rows + 16, LANES), F32)
    sign = pltpu.VMEM((rows, LANES), F32)
    row, layer = shape((layers, depth), BF16), shape((rows, depth), BF16)
    first_row, last_row, first_layer, last_layer = call(edge_kernel, (volume,), (row, row, layer, layer), [], "edges")
    above = lax.ppermute(last_row, "by", up_y)
    below = lax.ppermute(first_row, "by", down_y)
    before = lax.ppermute(last_layer, "bx", up_x)
    after = lax.ppermute(first_layer, "bx", down_x)
    busy = pl.CostEstimate(flops=40 * layers * half * depth, bytes_accessed=2 * layers * rows * depth, transcendentals=0)
    part = call(
        functools.partial(inner_kernel, layers * size_x),
        (volume, view),
        shape((5, half, depth), F32),
        [field, field, sign],
        "inner",
        busy,
    )
    codes = call(
        functools.partial(outer_kernel, layers * size_x),
        (volume, before, after, above, below, view, part),
        shape((size_x, 4, half, LANES), jnp.int16),
        [field, field, sign, pltpu.VMEM((4, rows, depth), F32)],
        "outer",
        busy,
    )
    codes = lax.all_to_all(codes, "bx", split_axis=0, concat_axis=0, tiled=True)
    return call(fold_kernel, (codes, view), shape((4, rows, depth // size_x), F32), [], "fold")


def solution(mesh):
    placed = (P("bx", "by", None), P("by"))
    return jax.shard_map(body, mesh=mesh, in_specs=placed, out_specs=P(None, "by", "bx"), check_vma=False)
```

```python
import functools
import math

import jax
import jax.numpy as jnp
from jax import lax
from jax.experimental import pallas as pl
from jax.experimental.pallas import tpu as pltpu
from jax.sharding import PartitionSpec as P

F32 = jnp.float32
BF16 = jnp.bfloat16
LANES = 128
TILES = 8
LOG2E = 1.0 / math.log(2.0)
FLOOR = -27.0
STEPS = 2621.0
TONE = 0.7 * 0.48 * 0.48


def recip(x):
    return pl.reciprocal(x, approx=True)


def lane_tile(start):
    return pl.ds(pl.multiple_of(start, LANES), LANES)


def encode(value):
    level = jnp.log2(jnp.maximum(value, 2.0**FLOOR)) * STEPS + (0.5 - FLOOR * STEPS)
    return level.astype(jnp.int32) - 32768


def decode(code):
    code = code.astype(jnp.int32)
    value = jnp.exp2(code.astype(F32) * (1.0 / STEPS) + (32768.0 / STEPS + FLOOR))
    return jnp.where(code == -32768, 0.0, value)


def side_column(view):
    rows = view.shape[1]
    spread = jnp.broadcast_to(view[...].astype(F32), (rows, rows))
    down = lax.broadcasted_iota(jnp.int32, (rows, rows), 0)
    along = lax.broadcasted_iota(jnp.int32, (rows, rows), 1)
    picked = jnp.sum(jnp.where(down == along, spread, 0.0), axis=1, keepdims=True)
    return jnp.where(picked > 0.5, 1.0, -1.0)


def edge_kernel(vol, first_row, last_row, first_layer, last_layer):
    layers, rows, depth = vol.shape

    def tile(z, carry):
        here = lane_tile(LANES * z)
        first_row[:, here] = jnp.concatenate([vol[l, :, here].astype(F32)[:1] for l in range(layers)], 0).astype(BF16)
        last_row[:, here] = jnp.concatenate([vol[l, :, here].astype(F32)[rows - 1 :] for l in range(layers)], 0).astype(BF16)
        first_layer[:, here] = vol[0, :, here]
        last_layer[:, here] = vol[layers - 1, :, here]
        return carry

    lax.fori_loop(0, depth // LANES, tile, 0, unroll=2)


class March:
    def __init__(self, field, ray_length, group):
        self.field, self.group = field, group
        self.lane = lax.broadcasted_iota(jnp.int32, (8, LANES), 1)
        self.row = lax.broadcasted_iota(jnp.int32, (8, LANES), 0)

    def tile(self, t):
        return self.group * TILES + t

    def here(self, t):
        return lane_tile(LANES * self.tile(t))

    def at(self, l, t, row):
        return self.field[l, self.tile(t) + 1, pl.ds(row, 8), :]

    def fresh(self):
        return dict(
            path=[jnp.zeros((8, LANES), F32) for _ in range(TILES)],
            reach=[jnp.ones((8, LANES), F32) for _ in range(TILES)],
            color=[[jnp.zeros((8, LANES), F32) for _ in range(TILES)] for _ in range(4)],
        )

    def layer(self, r, l, rate, state, before=None, after=None, above=None, below=None):
        lane, r8 = self.lane, 8 * r
        path, reach, color = state["path"], state["reach"], state["color"]
        mid = [self.at(l, t, r8) for t in range(-1, TILES + 1)]
        from_left = [pltpu.roll(v, 1, 1) for v in mid[:-1]]
        from_right = [pltpu.roll(v, LANES - 1, 1) for v in mid[1:]]
        for t in range(TILES):
            v = mid[t + 1]
            if above is None:
                up = self.at(l, t, r8 - 1)
            else:
                up = jnp.where(self.row == 0, above[pl.ds(l, 1), self.here(t)], pltpu.roll(v, 1, 0))
            if below is None:
                down = self.at(l, t, r8 + 1)
            else:
                down = jnp.where(self.row == 7, below[pl.ds(l, 1), self.here(t)], pltpu.roll(v, 7, 0))
            back = self.at(l - 1, t, r8) if before is None else edge_rows(before, r, self.here(t))
            front = self.at(l + 1, t, r8) if after is None else edge_rows(after, r, self.here(t))
            gx = front - back
            gy = down - up
            gz = jnp.where(lane == LANES - 1, from_right[t + 1], from_right[t]) - jnp.where(
                lane == 0, from_left[t], from_left[t + 1]
            )
            square = gx * gx + gy * gy + gz * gz
            facing = gx + (0.6 / 0.48) * gy + (0.64 / 0.48) * gz
            shading = 0.3 / TONE + facing * facing * recip(square + 4.0)
            lifted = jnp.maximum(v, 0.4)
            density = jnp.minimum(lifted, 1.6) - 0.4
            path[t] = path[t] + density * (rate[0][...] - rate[1][...] * recip(square + 1.0))
            next_reach = jnp.exp2(path[t])
            weight = (next_reach - reach[t]) * shading
            reach[t] = next_reach
            color[0][t] = color[0][t] + weight * jnp.clip(v, 0.8, 1.8)
            color[1][t] = color[1][t] + weight * jnp.minimum(v, 2.0 - v)
            color[2][t] = color[2][t] + weight * jnp.minimum(lifted, 1.2)
            color[3][t] = color[3][t] + weight


def edge_rows(layer, r, here):
    return layer[pl.ds(16 * (r // 2), 16), here].astype(F32)[8 * (r % 2) : 8 * (r % 2) + 8]


def set_rates(view, ray_length, rates):
    rows = rates.shape[1]
    side = jnp.broadcast_to(side_column(view), (rows, LANES))
    scale = 3.0 / 1.2 / ray_length * LOG2E
    rates[0] = side * (1.25 * scale)
    rates[1] = side * scale


def rates_of(rates, r):
    return rates.at[0, pl.ds(8 * r, 8)], rates.at[1, pl.ds(8 * r, 8)]


def inner_kernel(ray_length, vol, view, part, field, rates):
    layers, rows, depth = vol.shape
    tiles = depth // LANES
    set_rates(view, ray_length, rates)

    def widen(l, carry):
        field[l, 0] = jnp.zeros((rows, LANES), F32)
        field[l, tiles + 1] = jnp.zeros((rows, LANES), F32)
        for tile in range(tiles):
            field[l, tile + 1] = vol[l, :, pl.ds(LANES * tile, LANES)].astype(F32)
        return carry

    lax.fori_loop(0, layers, widen, 0)

    def work(group, carry):
        march = March(field, ray_length, group)
        for r in (1, 2):
            state = march.fresh()
            for l in range(1, layers - 1):
                march.layer(r, l, rates_of(rates, r), state)
            for t in range(TILES):
                for k, kind in enumerate([state["path"]] + state["color"]):
                    part[k, pl.ds(8 * r - 8, 8), march.here(t)] = kind[t]
        return carry

    lax.fori_loop(0, tiles // TILES, work, 0)


def outer_kernel(ray_length, before, after, above, below, view, part, field, codes, rates, above_wide, below_wide, levels):
    layers, _, rows, _ = field.shape
    tiles = part.shape[2] // LANES
    set_rates(view, ray_length, rates)
    above_wide[...] = above[...].astype(F32)
    below_wide[...] = below[...].astype(F32)
    half = rows // 2

    def work(group, carry):
        march = March(field, ray_length, group)

        def finish(r, state):
            side = rates[1, pl.ds(8 * r, 8)]
            for t in range(TILES):
                path = state["path"][t]
                red, green, blue, total = (kind[t] for kind in state["color"])
                factor = jnp.where(side > 0, jnp.exp2(-path), -1.0) * TONE
                final = [(red - 0.8 * total) * factor, green * factor, (1.2 * total - blue) * factor, jnp.abs(path)]
                for k in range(4):
                    levels[k, t, pl.ds(8 * r, 8), :] = encode(final[k])

        for r in (0, 3):
            rate = rates_of(rates, r)
            state = march.fresh()
            for l in range(layers):
                march.layer(
                    r,
                    l,
                    rate,
                    state,
                    before if l == 0 else None,
                    after if l == layers - 1 else None,
                    above_wide if r == 0 else None,
                    below_wide if r == 3 else None,
                )
            finish(r, state)
        for r in (1, 2):
            rate = rates_of(rates, r)
            state = march.fresh()
            march.layer(r, 0, rate, state, before=before)
            for t in range(TILES):
                block = [part[k, pl.ds(8 * r - 8, 8), march.here(t)] for k in range(5)]
                for k in range(4):
                    state["color"][k][t] = state["color"][k][t] + state["reach"][t] * block[k + 1]
                state["path"][t] = state["path"][t] + block[0]
                state["reach"][t] = jnp.exp2(state["path"][t])
            march.layer(r, layers - 1, rate, state, after=after)
            finish(r, state)
        low = lax.broadcasted_iota(jnp.int32, (half, LANES), 1) < LANES // 2
        for t in range(TILES):
            z = march.tile(t)
            for k in range(4):
                top, bottom = levels[k, t, pl.ds(0, half)], levels[k, t, pl.ds(half, half)]
                codes[2 * z, k] = jnp.where(low, top, pltpu.roll(bottom, LANES // 2, 1)).astype(jnp.int16)
                codes[2 * z + 1, k] = jnp.where(low, pltpu.roll(top, LANES // 2, 1), bottom).astype(jnp.int16)
        return carry

    lax.fori_loop(0, tiles // TILES, work, 0)


def fold_kernel(codes, view, out):
    bricks, _, half, _ = codes.shape
    column = side_column(view)
    low = lax.broadcasted_iota(jnp.int32, (half, LANES), 1) < LANES // 2
    side = jnp.where(low, column[:half], column[half:])
    backward = side > 0
    path = jnp.zeros((half, LANES), F32)
    color = [jnp.zeros((half, LANES), F32) for _ in range(3)]
    for k in range(bricks):
        farther = path + decode(codes[k, 3])
        reach = jnp.exp2(side * jnp.where(backward, farther, path))
        path = farther
        for q in range(3):
            color[q] = color[q] + reach * decode(codes[k, q])
    passing = jnp.exp2(-path)
    factor = jnp.where(backward, passing, 1.0)
    parts = [c * factor for c in color] + [1.0 - passing]
    for q in range(4):
        out[q, pl.ds(0, half), :] = parts[q][:, : LANES // 2]
        out[q, pl.ds(half, half), :] = parts[q][:, LANES // 2 :]


def body(volume, view_side):
    layers, rows, depth = volume.shape
    size_x, size_y = lax.axis_size("bx"), lax.axis_size("by")
    up_x = [(i, i + 1) for i in range(size_x - 1)]
    up_y = [(i, i + 1) for i in range(size_y - 1)]
    down_x = [(j, i) for i, j in up_x]
    down_y = [(j, i) for i, j in up_y]
    view = view_side[None, :]
    half = rows // 2
    in_vmem = pl.BlockSpec(memory_space=pltpu.VMEM)
    shape = jax.ShapeDtypeStruct

    def call(kernel, operands, out_shape, scratch, name, cost=None, limit=24):
        return pl.pallas_call(
            kernel,
            out_shape=out_shape,
            in_specs=[in_vmem] * len(operands),
            out_specs=jax.tree.map(lambda _: in_vmem, out_shape),
            scratch_shapes=scratch,
            compiler_params=pltpu.CompilerParams(vmem_limit_bytes=limit << 20),
            cost_estimate=cost,
            name=name,
        )(*operands)

    rates = pltpu.VMEM((2, rows, LANES), F32)
    row, layer = shape((layers, depth), BF16), shape((rows, depth), BF16)
    first_row, last_row, first_layer, last_layer = call(edge_kernel, (volume,), (row, row, layer, layer), [], "edges")
    above = lax.ppermute(last_row, "by", up_y)
    below = lax.ppermute(first_row, "by", down_y)
    before = lax.ppermute(last_layer, "bx", up_x)
    after = lax.ppermute(first_layer, "bx", down_x)
    busy = pl.CostEstimate(flops=40 * layers * half * depth, bytes_accessed=2 * layers * rows * depth, transcendentals=0)
    part, field = call(
        functools.partial(inner_kernel, layers * size_x),
        (volume, view),
        (shape((5, half, depth), F32), shape((layers, depth // LANES + 2, rows, LANES), F32)),
        [rates],
        "inner",
        busy,
    )
    wide = pltpu.VMEM((layers, depth), F32)
    codes = call(
        functools.partial(outer_kernel, layers * size_x),
        (before, after, above, below, view, part, field),
        shape((size_x, 4, half, LANES), jnp.int16),
        [rates, wide, wide, pltpu.VMEM((4, TILES, rows, LANES), jnp.int32)],
        "outer",
        busy,
    )
    codes = lax.all_to_all(codes, "bx", split_axis=0, concat_axis=0, tiled=True)
    return call(fold_kernel, (codes, view), shape((4, rows, depth // size_x), F32), [], "fold")


def solution(mesh):
    placed = (P("bx", "by", None), P("by"))
    return jax.shard_map(body, mesh=mesh, in_specs=placed, out_specs=P(None, "by", "bx"), check_vma=False)
```

```python
import functools
import math

import jax
import jax.numpy as jnp
from jax import lax
from jax.experimental import pallas as pl
from jax.experimental.pallas import tpu as pltpu
from jax.sharding import PartitionSpec as P

F32 = jnp.float32
BF16 = jnp.bfloat16
LANES = 128
TILES = 8
LOG2E = 1.0 / math.log(2.0)
FLOOR = -27.0
STEPS = 2570.0
TONE = 0.7 * 0.48 * 0.48


def recip(x):
    return pl.reciprocal(x, approx=True)


def lane_tile(start):
    return pl.ds(pl.multiple_of(start, LANES), LANES)


def encode(value):
    level = jnp.log2(jnp.maximum(value, 2.0**FLOOR)) * STEPS + (0.5 - FLOOR * STEPS)
    return level.astype(jnp.int32) - 32768


def decode(code):
    code = code.astype(jnp.int32)
    value = jnp.exp2(code.astype(F32) * (1.0 / STEPS) + (32768.0 / STEPS + FLOOR))
    return jnp.where(code == -32768, 0.0, value)


def core_index():
    return lax.rem(lax.axis_index("bx"), 2)


def side_column(view):
    rows = view.shape[1]
    spread = jnp.broadcast_to(view[...].astype(F32), (rows, rows))
    down = lax.broadcasted_iota(jnp.int32, (rows, rows), 0)
    along = lax.broadcasted_iota(jnp.int32, (rows, rows), 1)
    picked = jnp.sum(jnp.where(down == along, spread, 0.0), axis=1, keepdims=True)
    return jnp.where(picked > 0.5, 1.0, -1.0)


def one_row(ref, row, here):
    return jnp.concatenate([ref[l, :, here].astype(F32)[row : row + 1] for l in range(16)], 0).astype(BF16)


def share_kernel(vol, send, keep):
    layers, rows, depth = vol.shape
    half = rows // 2

    def share(far, sent_row, kept_row):
        def tile(z, carry):
            here = lane_tile(LANES * z)
            for l in range(layers):
                send[l, :, here] = vol[l, pl.ds(far, half), here]
            send[layers, :, here] = one_row(vol, sent_row, here)
            keep[:, here] = one_row(vol, kept_row, here)
            return carry

        lax.fori_loop(0, depth // LANES, tile, 0, unroll=2)

    core = core_index()

    @pl.when(core == 0)
    def _():
        share(half, half - 1, half)

    @pl.when(core == 1)
    def _():
        share(0, half, half - 1)


def face_kernel(vol, mate, own, first, last, rim):
    layers, rows, depth = vol.shape
    half = rows // 2
    core = core_index()

    @pl.when(core == 0)
    def _():
        def tile(z, carry):
            here = lane_tile(LANES * z)
            first[:, here] = vol[0, pl.ds(0, half), here]
            last[:, here] = mate[layers - 1, :, here]
            rim[pl.ds(0, layers), here] = one_row(vol, 0, here)
            rim[pl.ds(layers, layers), here] = one_row(mate, 0, here)
            return carry

        lax.fori_loop(0, depth // LANES, tile, 0, unroll=2)

    @pl.when(core == 1)
    def _():
        def tile(z, carry):
            here = lane_tile(LANES * z)
            first[:, here] = mate[0, :, here]
            last[:, here] = vol[layers - 1, pl.ds(half, half), here]
            rim[pl.ds(0, layers), here] = one_row(mate, half - 1, here)
            rim[pl.ds(layers, layers), here] = one_row(vol, rows - 1, here)
            return carry

        lax.fori_loop(0, depth // LANES, tile, 0, unroll=2)


class March:
    def __init__(self, field, group):
        self.field, self.group = field, group
        self.lane = lax.broadcasted_iota(jnp.int32, (8, LANES), 1)

    def tile(self, t):
        return self.group * TILES + t

    def here(self, t):
        return lane_tile(LANES * self.tile(t))

    def at(self, l, t, row):
        return self.field[l, self.tile(t) + 1, pl.ds(row, 8), :]

    def fresh(self):
        return dict(
            path=[jnp.zeros((8, LANES), F32) for _ in range(TILES)],
            reach=[jnp.ones((8, LANES), F32) for _ in range(TILES)],
            color=[[jnp.zeros((8, LANES), F32) for _ in range(TILES)] for _ in range(4)],
        )

    def layer(self, row, l, rate, state, before=None, after=None, rim=None):
        lane = self.lane
        path, reach, color = state["path"], state["reach"], state["color"]
        mid = [self.at(l, t, row) for t in range(-1, TILES + 1)]
        from_left = [pltpu.roll(v, 1, 1) for v in mid[:-1]]
        from_right = [pltpu.roll(v, LANES - 1, 1) for v in mid[1:]]
        for t in range(TILES):
            v = mid[t + 1]
            up, down = self.at(l, t, row - 1), self.at(l, t, row + 1)
            if rim is not None:
                beyond = jnp.broadcast_to(rim[0][pl.ds(l, 1), self.here(t)], (8, LANES))
                up, down = jnp.where(rim[1], beyond, up), jnp.where(rim[2], beyond, down)
            back = self.at(l - 1, t, row) if before is None else before[:, self.here(t)]
            front = self.at(l + 1, t, row) if after is None else after[:, self.here(t)]
            gx = front - back
            gy = down - up
            gz = jnp.where(lane == LANES - 1, from_right[t + 1], from_right[t]) - jnp.where(
                lane == 0, from_left[t], from_left[t + 1]
            )
            square = gx * gx + gy * gy + gz * gz
            facing = gx + (0.6 / 0.48) * gy + (0.64 / 0.48) * gz
            shading = 0.3 / TONE + facing * facing * recip(square + 4.0)
            lifted = jnp.maximum(v, 0.4)
            density = jnp.minimum(lifted, 1.6) - 0.4
            path[t] = path[t] + density * (rate[0][...] - rate[1][...] * recip(square + 1.0))
            next_reach = jnp.exp2(path[t])
            weight = (next_reach - reach[t]) * shading
            reach[t] = next_reach
            color[0][t] = color[0][t] + weight * jnp.clip(v, 0.8, 1.8)
            color[1][t] = color[1][t] + weight * jnp.minimum(v, 2.0 - v)
            color[2][t] = color[2][t] + weight * jnp.minimum(lifted, 1.2)
            color[3][t] = color[3][t] + weight

    def keep(self, state, part):
        for t in range(TILES):
            for k, kind in enumerate([state["path"]] + state["color"]):
                part[k, :, self.here(t)] = kind[t]


def set_rates(view, ray_length, rates):
    rows = rates.shape[1]
    side = jnp.broadcast_to(side_column(view), (rows, LANES))
    scale = 3.0 / 1.2 / ray_length * LOG2E
    rates[0] = side * (1.25 * scale)
    rates[1] = side * scale


def rates_of(rates, row):
    here = pl.ds(pl.multiple_of(row, 8), 8)
    return rates.at[0, here], rates.at[1, here]


def own_kernel(ray_length, vol, view, part, field, rates):
    layers, rows, depth = vol.shape
    tiles = depth // LANES
    set_rates(view, ray_length, rates)

    def widen(l, carry):
        field[l, 0] = jnp.zeros((rows, LANES), F32)
        field[l, tiles + 1] = jnp.zeros((rows, LANES), F32)
        for tile in range(tiles):
            field[l, tile + 1] = vol[l, :, pl.ds(LANES * tile, LANES)].astype(F32)
        return carry

    lax.fori_loop(0, layers, widen, 0)
    row = pl.multiple_of(8 + 8 * core_index(), 8)

    def work(group, carry):
        march = March(field, group)
        state = march.fresh()
        for l in range(1, layers - 1):
            march.layer(row, l, rates_of(rates, row), state)
        march.keep(state, part)
        return carry

    lax.fori_loop(0, tiles // TILES, work, 0)


def mate_kernel(ray_length, vol, mate, keep, view, part, field, rates):
    layers, rows, depth = vol.shape
    tiles, half = depth // LANES, rows // 2
    set_rates(view, ray_length, rates)
    core = core_index()
    inside = pl.ds(8, half)
    mine, other = layers * core, layers * (1 - core)
    own_rows = pl.ds(pl.multiple_of(half * core, half), half)

    def widen(l, carry):
        for index in (mine + l, other + l):
            field[index, 0, inside, :] = jnp.zeros((half, LANES), F32)
            field[index, tiles + 1, inside, :] = jnp.zeros((half, LANES), F32)
        for tile in range(tiles):
            here = pl.ds(LANES * tile, LANES)
            field[mine + l, tile + 1, inside, :] = vol[l, own_rows, here].astype(F32)
            field[other + l, tile + 1, inside, :] = mate[l, :, here].astype(F32)
        return carry

    lax.fori_loop(0, layers, widen, 0)

    def border(slot, mine, other):
        def tile(z, carry):
            here = lane_tile(LANES * z)
            field[pl.ds(mine, layers), z + 1, slot, :] = keep[:, here].astype(F32)
            field[pl.ds(other, layers), z + 1, slot, :] = mate[layers, :, here].astype(F32)
            return carry

        lax.fori_loop(0, tiles, tile, 0, unroll=2)

    @pl.when(core == 0)
    def _():
        border(half + 8, 0, layers)

    @pl.when(core == 1)
    def _():
        border(7, layers, 0)

    row = pl.multiple_of(16 - 8 * core, 8)
    begin = layers - 1 - (layers - 2) * core

    def work(group, carry):
        march = March(field, group)
        state = march.fresh()
        for k in range(layers):
            march.layer(row, begin + k, rates_of(rates, 8 + 8 * core), state)
        march.keep(state, part)
        return carry

    lax.fori_loop(0, tiles // TILES, work, 0)


def rim_masks(core):
    rows_down = lax.broadcasted_iota(jnp.int32, (8, LANES), 0)
    return rows_down == 8 * core, rows_down == 8 - core


def rim_kernel(ray_length, beyond, view, field, part, rates, beyond_wide):
    layers = field.shape[0]
    tiles = part.shape[2] // LANES
    set_rates(view, ray_length, rates)
    beyond_wide[...] = beyond[...].astype(F32)
    core = core_index()
    above, below = rim_masks(core)
    row = pl.multiple_of(8 + 8 * core, 8)

    def work(group, carry):
        march = March(field, group)
        state = march.fresh()
        for l in range(1, layers - 1):
            march.layer(row, l, rates_of(rates, 24 * core), state, rim=(beyond_wide, above, below))
        march.keep(state, part)
        return carry

    lax.fori_loop(0, tiles // TILES, work, 0)


def outer_kernel(ray_length, before, after, beyond, view, own, other, border, field, codes, rates, before_wide, after_wide, beyond_wide, levels):
    layers = field.shape[0]
    tiles = own.shape[2] // LANES
    set_rates(view, ray_length, rates)
    before_wide[...] = before[...].astype(F32)
    after_wide[...] = after[...].astype(F32)
    beyond_wide[...] = beyond[...].astype(F32)
    core = core_index()
    above, below = rim_masks(core)
    own_first = jnp.zeros((8, LANES), jnp.int32) + core == 0
    low = lax.broadcasted_iota(jnp.int32, (8, LANES), 1) < LANES // 2

    def work(group, carry):
        march = March(field, group)

        def column(place, rate, blocks, rim):
            place = pl.multiple_of(place, 8)
            row = pl.multiple_of(8 + place, 8)
            state = march.fresh()
            march.layer(row, 0, rate, state, before=before_wide.at[pl.ds(place, 8)], rim=rim)
            for t in range(TILES):
                for block in blocks(t):
                    for k in range(4):
                        state["color"][k][t] = state["color"][k][t] + state["reach"][t] * block[k + 1]
                    state["path"][t] = state["path"][t] + block[0]
                    state["reach"][t] = jnp.exp2(state["path"][t])
            march.layer(row, layers - 1, rate, state, after=after_wide.at[pl.ds(place, 8)], rim=rim)
            side = rate[1][...]
            for t in range(TILES):
                path = state["path"][t]
                red, green, blue, total = (kind[t] for kind in state["color"])
                factor = jnp.where(side > 0, jnp.exp2(-path), -1.0) * TONE
                final = [(red - 0.8 * total) * factor, green * factor, (1.2 * total - blue) * factor, jnp.abs(path)]
                for k in range(4):
                    levels[k, t, pl.ds(place, 8), :] = encode(final[k])

        def outside(t):
            return [[border[k, :, march.here(t)] for k in range(5)]]

        def inside(t):
            mine = [own[k, :, march.here(t)] for k in range(5)]
            others = [other[k, :, march.here(t)] for k in range(5)]
            return (
                [jnp.where(own_first, a, b) for a, b in zip(mine, others)],
                [jnp.where(own_first, b, a) for a, b in zip(mine, others)],
            )

        column(8 * core, rates_of(rates, 24 * core), outside, (beyond_wide, above, below))
        column(8 - 8 * core, rates_of(rates, 8 + 8 * core), inside, None)
        for t in range(TILES):
            z = march.tile(t)
            even, odd = [], []
            for k in range(4):
                top, bottom = levels[k, t, pl.ds(0, 8)], levels[k, t, pl.ds(8, 8)]
                even.append(jnp.where(low, top, pltpu.roll(bottom, LANES // 2, 1)))
                odd.append(jnp.where(low, pltpu.roll(top, LANES // 2, 1), bottom))
            for k in range(2):
                codes[2 * z, k] = jnp.concatenate(even[2 * k : 2 * k + 2], 0).astype(jnp.int16)
                codes[2 * z + 1, k] = jnp.concatenate(odd[2 * k : 2 * k + 2], 0).astype(jnp.int16)
        return carry

    lax.fori_loop(0, tiles // TILES, work, 0)


def fold_kernel(codes, view, out):
    bricks = codes.shape[0]
    column = side_column(view)
    low = lax.broadcasted_iota(jnp.int32, (8, LANES), 1) < LANES // 2
    for core in range(2):
        base = 16 * core
        side = jnp.where(low, column[base : base + 8], column[base + 8 : base + 16])
        backward = side > 0
        path = jnp.zeros((8, LANES), F32)
        color = [jnp.zeros((8, LANES), F32) for _ in range(3)]
        for k in range(core, bricks, 2):
            values = [decode(codes[k, 0]), decode(codes[k, 1])]
            farther = path + values[1][8:]
            reach = jnp.exp2(side * jnp.where(backward, farther, path))
            path = farther
            color[0] = color[0] + reach * values[0][:8]
            color[1] = color[1] + reach * values[0][8:]
            color[2] = color[2] + reach * values[1][:8]
        passing = jnp.exp2(-path)
        factor = jnp.where(backward, passing, 1.0)
        parts = [c * factor for c in color] + [1.0 - passing]
        for q in range(4):
            out[q, pl.ds(base, 8), :] = parts[q][:, : LANES // 2]
            out[q, pl.ds(base + 8, 8), :] = parts[q][:, LANES // 2 :]


def body(volume, view_side):
    layers, rows, depth = volume.shape
    size_x, size_y = lax.axis_size("bx"), lax.axis_size("by")
    half = rows // 2
    mates = [(i, i ^ 1) for i in range(size_x)]
    up_x = [(i, i + 2) for i in range(size_x - 2)]
    down_x = [(j, i) for i, j in up_x]
    across = []
    for i in range(0, size_x, 2):
        for j in range(size_y - 1):
            upper, lower = (i + 1) * size_y + j, i * size_y + j + 1
            across += [(upper, lower), (lower, upper)]
    view = view_side[None, :]
    in_vmem = pl.BlockSpec(memory_space=pltpu.VMEM)
    shape = jax.ShapeDtypeStruct

    def call(kernel, operands, out_shape, scratch, name, cost=0, limit=24):
        return pl.pallas_call(
            kernel,
            out_shape=out_shape,
            in_specs=[in_vmem] * len(operands),
            out_specs=jax.tree.map(lambda _: in_vmem, out_shape),
            scratch_shapes=scratch,
            compiler_params=pltpu.CompilerParams(vmem_limit_bytes=limit << 20),
            cost_estimate=pl.CostEstimate(flops=cost, bytes_accessed=2 * layers * rows * depth, transcendentals=0) if cost else None,
            name=name,
        )(*operands)

    work = 40 * layers * half * depth
    length = layers * size_x
    rates = pltpu.VMEM((2, rows, LANES), F32)
    face, part = shape((half, depth), BF16), shape((5, 8, depth), F32)
    send, keep = call(share_kernel, (volume,), (shape((layers + 1, half, depth), BF16), face), [], "share")
    mate = lax.ppermute(send, "bx", mates)
    own = call(
        functools.partial(own_kernel, length),
        (volume, view),
        part,
        [pltpu.VMEM((layers, depth // LANES + 2, rows, LANES), F32), rates],
        "own",
        work // 2,
    )
    first, last, rim = call(face_kernel, (volume, mate, own), (face, face, shape((2 * layers, depth), BF16)), [], "face")
    beyond = lax.ppermute(rim, ("bx", "by"), across)
    before = lax.ppermute(last, "bx", up_x)
    after = lax.ppermute(first, "bx", down_x)
    other, field = call(
        functools.partial(mate_kernel, length),
        (volume, mate, keep, view),
        (part, shape((2 * layers, depth // LANES + 2, half + 16, LANES), F32)),
        [rates],
        "mate",
        work // 2,
    )
    wide, rim_wide = pltpu.VMEM((half, depth), F32), pltpu.VMEM((2 * layers, depth), F32)
    border = call(functools.partial(rim_kernel, length), (beyond, view, field), part, [rates, rim_wide], "rim", work)
    codes = call(
        functools.partial(outer_kernel, length),
        (before, after, beyond, view, own, other, border, field),
        shape((size_x, 2, 16, LANES), jnp.int16),
        [rates, wide, wide, rim_wide, pltpu.VMEM((4, TILES, 16, LANES), jnp.int32)],
        "outer",
        work,
    )
    codes = lax.all_to_all(codes, "bx", split_axis=0, concat_axis=0, tiled=True)
    return call(fold_kernel, (codes, view), shape((4, rows, depth // size_x), F32), [], "fold")


def solution(mesh):
    placed = (P("bx", "by", None), P("by"))
    return jax.shard_map(body, mesh=mesh, in_specs=placed, out_specs=P(None, "by", "bx"), check_vma=False)
```

```python
import functools
import math

import jax
import jax.numpy as jnp
from jax import lax
from jax.experimental import pallas as pl
from jax.experimental.pallas import tpu as pltpu
from jax.sharding import PartitionSpec as P

F32 = jnp.float32
BF16 = jnp.bfloat16
LANES = 128
TILES = 8
LOG2E = 1.0 / math.log(2.0)
FLOOR = -27.0
STEPS = 2570.0
TONE = 0.7 * 0.48 * 0.48


def recip(x):
    return pl.reciprocal(x, approx=True)


def lane_tile(start):
    return pl.ds(pl.multiple_of(start, LANES), LANES)


def encode(value):
    level = jnp.log2(jnp.maximum(value, 2.0**FLOOR)) * STEPS + (0.5 - FLOOR * STEPS)
    return level.astype(jnp.int32) - 32768


def decode(code):
    code = code.astype(jnp.int32)
    value = jnp.exp2(code.astype(F32) * (1.0 / STEPS) + (32768.0 / STEPS + FLOOR))
    return jnp.where(code == -32768, 0.0, value)


def core_index():
    return lax.rem(lax.axis_index("bx"), 2)


def side_column(view):
    rows = view.shape[1]
    spread = jnp.broadcast_to(view[...].astype(F32), (rows, rows))
    down = lax.broadcasted_iota(jnp.int32, (rows, rows), 0)
    along = lax.broadcasted_iota(jnp.int32, (rows, rows), 1)
    picked = jnp.sum(jnp.where(down == along, spread, 0.0), axis=1, keepdims=True)
    return jnp.where(picked > 0.5, 1.0, -1.0)


def one_row(ref, row, here):
    return jnp.concatenate([ref[l, :, here].astype(F32)[row : row + 1] for l in range(16)], 0).astype(BF16)


def share_kernel(vol, send):
    layers, rows, depth = vol.shape
    half = rows // 2

    def share(far, row):
        def tile(z, carry):
            here = lane_tile(LANES * z)
            for l in range(layers):
                send[l, :, here] = vol[l, pl.ds(far, half), here]
            send[layers, :, here] = one_row(vol, row, here)
            return carry

        lax.fori_loop(0, depth // LANES, tile, 0, unroll=2)

    core = core_index()

    @pl.when(core == 0)
    def _():
        share(half, half - 1)

    @pl.when(core == 1)
    def _():
        share(0, half)


def own_faces(vol, core, end, rim):
    layers, rows, depth = vol.shape
    half = rows // 2

    def faces(layer, first, row):
        def tile(z, carry):
            here = lane_tile(LANES * z)
            end[:, here] = vol[layer, pl.ds(first, half), here]
            rim[:, here] = one_row(vol, row, here)
            return carry

        lax.fori_loop(0, depth // LANES, tile, 0, unroll=2)

    @pl.when(core == 0)
    def _():
        faces(0, 0, 0)

    @pl.when(core == 1)
    def _():
        faces(layers - 1, half, rows - 1)


def face_kernel(mate, own_end, own_rim, first, last, rim):
    layers, half, depth = mate.shape[0] - 1, mate.shape[1], mate.shape[2]
    core = core_index()

    @pl.when(core == 0)
    def _():
        def tile(z, carry):
            here = lane_tile(LANES * z)
            first[:, here] = own_end[:, here]
            last[:, here] = mate[layers - 1, :, here]
            rim[pl.ds(0, layers), here] = own_rim[:, here]
            rim[pl.ds(layers, layers), here] = one_row(mate, 0, here)
            return carry

        lax.fori_loop(0, depth // LANES, tile, 0, unroll=4)

    @pl.when(core == 1)
    def _():
        def tile(z, carry):
            here = lane_tile(LANES * z)
            first[:, here] = mate[0, :, here]
            last[:, here] = own_end[:, here]
            rim[pl.ds(0, layers), here] = one_row(mate, half - 1, here)
            rim[pl.ds(layers, layers), here] = own_rim[:, here]
            return carry

        lax.fori_loop(0, depth // LANES, tile, 0, unroll=4)


class March:
    def __init__(self, field, group):
        self.field, self.group = field, group
        self.lane = lax.broadcasted_iota(jnp.int32, (8, LANES), 1)

    def tile(self, t):
        return self.group * TILES + t

    def here(self, t):
        return lane_tile(LANES * self.tile(t))

    def at(self, l, t, row):
        return self.field[l, self.tile(t) + 1, pl.ds(row, 8), :]

    def fresh(self):
        return dict(
            path=[jnp.zeros((8, LANES), F32) for _ in range(TILES)],
            reach=[jnp.ones((8, LANES), F32) for _ in range(TILES)],
            color=[[jnp.zeros((8, LANES), F32) for _ in range(TILES)] for _ in range(4)],
        )

    def layer(self, row, l, rate, state, before=None, after=None, rim=None):
        lane = self.lane
        path, reach, color = state["path"], state["reach"], state["color"]
        mid = [self.at(l, t, row) for t in range(-1, TILES + 1)]
        from_left = [pltpu.roll(v, 1, 1) for v in mid[:-1]]
        from_right = [pltpu.roll(v, LANES - 1, 1) for v in mid[1:]]
        for t in range(TILES):
            v = mid[t + 1]
            up, down = self.at(l, t, row - 1), self.at(l, t, row + 1)
            if rim is not None:
                beyond = jnp.broadcast_to(rim[0][pl.ds(l, 1), self.here(t)], (8, LANES))
                up, down = jnp.where(rim[1], beyond, up), jnp.where(rim[2], beyond, down)
            back = self.at(l - 1, t, row) if before is None else before[:, self.here(t)]
            front = self.at(l + 1, t, row) if after is None else after[:, self.here(t)]
            gx = front - back
            gy = down - up
            gz = jnp.where(lane == LANES - 1, from_right[t + 1], from_right[t]) - jnp.where(
                lane == 0, from_left[t], from_left[t + 1]
            )
            square = gx * gx + gy * gy + gz * gz
            facing = gx + (0.6 / 0.48) * gy + (0.64 / 0.48) * gz
            shading = 0.3 / TONE + facing * facing * recip(square + 4.0)
            lifted = jnp.maximum(v, 0.4)
            density = jnp.minimum(lifted, 1.6) - 0.4
            path[t] = path[t] + density * (rate[0][...] - rate[1][...] * recip(square + 1.0))
            next_reach = jnp.exp2(path[t])
            weight = (next_reach - reach[t]) * shading
            reach[t] = next_reach
            color[0][t] = color[0][t] + weight * jnp.clip(v, 0.8, 1.8)
            color[1][t] = color[1][t] + weight * jnp.minimum(v, 2.0 - v)
            color[2][t] = color[2][t] + weight * jnp.minimum(lifted, 1.2)
            color[3][t] = color[3][t] + weight

    def keep(self, state, part):
        for t in range(TILES):
            for k, kind in enumerate([state["path"]] + state["color"]):
                part[k, :, self.here(t)] = kind[t]


def set_rates(view, ray_length, rates):
    rows = rates.shape[1]
    side = jnp.broadcast_to(side_column(view), (rows, LANES))
    scale = 3.0 / 1.2 / ray_length * LOG2E
    rates[0] = side * (1.25 * scale)
    rates[1] = side * scale


def rates_of(rates, row):
    here = pl.ds(pl.multiple_of(row, 8), 8)
    return rates.at[0, here], rates.at[1, here]


def own_kernel(ray_length, vol, view, part, field, rates, end, rim):
    layers, rows, depth = vol.shape
    tiles, half = depth // LANES, rows // 2
    set_rates(view, ray_length, rates)
    core = core_index()
    own_faces(vol, core, end, rim)
    mine = layers * core

    def widen(first, beside):
        def one(l, carry):
            field[mine + l, 0] = jnp.zeros((rows, LANES), F32)
            field[mine + l, tiles + 1] = jnp.zeros((rows, LANES), F32)
            for tile in range(tiles):
                here = pl.ds(LANES * tile, LANES)
                field[mine + l, tile + 1, pl.ds(8, half), :] = vol[l, pl.ds(first, half), here].astype(F32)
                near = vol[l, pl.ds(half - first, half), here].astype(F32)
                field[mine + l, tile + 1, pl.ds(beside[1], 8), :] = near[beside[0] : beside[0] + 8]
            return carry

        lax.fori_loop(0, layers, one, 0)

    @pl.when(core == 0)
    def _():
        widen(0, (0, half + 8))

    @pl.when(core == 1)
    def _():
        widen(half, (half - 8, 0))

    row = pl.multiple_of(16 - 8 * core, 8)

    def work(group, carry):
        march = March(field, group)
        state = march.fresh()
        for l in range(1, layers - 1):
            march.layer(row, mine + l, rates_of(rates, 8 + 8 * core), state)
        march.keep(state, part)
        return carry

    lax.fori_loop(0, tiles // TILES, work, 0)


def mate_kernel(mate, rates, own_field, part, field):
    layers, half, depth = mate.shape[0] - 1, mate.shape[1], mate.shape[2]
    tiles = depth // LANES
    core = core_index()
    inside = pl.ds(8, half)
    other = layers * (1 - core)

    def widen(l, carry):
        field[other + l, 0, inside, :] = jnp.zeros((half, LANES), F32)
        field[other + l, tiles + 1, inside, :] = jnp.zeros((half, LANES), F32)
        for tile in range(tiles):
            field[other + l, tile + 1, inside, :] = mate[l, :, pl.ds(LANES * tile, LANES)].astype(F32)
        return carry

    lax.fori_loop(0, layers, widen, 0)

    def border(slot, other):
        def tile(z, carry):
            field[pl.ds(other, layers), z + 1, slot, :] = mate[layers, :, lane_tile(LANES * z)].astype(F32)
            return carry

        lax.fori_loop(0, tiles, tile, 0, unroll=2)

    @pl.when(core == 0)
    def _():
        border(half + 8, layers)

    @pl.when(core == 1)
    def _():
        border(7, 0)

    row = pl.multiple_of(16 - 8 * core, 8)
    begin = layers - 1 - (layers - 2) * core

    def work(group, carry):
        march = March(field, group)
        state = march.fresh()
        for k in range(layers):
            march.layer(row, begin + k, rates_of(rates, 8 + 8 * core), state)
        march.keep(state, part)
        return carry

    lax.fori_loop(0, tiles // TILES, work, 0)


def rim_masks(core):
    rows_down = lax.broadcasted_iota(jnp.int32, (8, LANES), 0)
    return rows_down == 8 * core, rows_down == 8 - core


def rim_kernel(beyond, rates, field, part, beyond_wide):
    layers = field.shape[0]
    tiles = part.shape[2] // LANES
    beyond_wide[...] = beyond[...].astype(F32)
    core = core_index()
    above, below = rim_masks(core)
    row = pl.multiple_of(8 + 8 * core, 8)

    def work(group, carry):
        march = March(field, group)
        state = march.fresh()
        for l in range(1, layers - 1):
            march.layer(row, l, rates_of(rates, 24 * core), state, rim=(beyond_wide, above, below))
        march.keep(state, part)
        return carry

    lax.fori_loop(0, tiles // TILES, work, 0)


def outer_kernel(before, after, beyond, rates, own, other, border, field, codes, before_wide, after_wide, beyond_wide, levels):
    layers = field.shape[0]
    tiles = own.shape[2] // LANES
    before_wide[...] = before[...].astype(F32)
    after_wide[...] = after[...].astype(F32)
    beyond_wide[...] = beyond[...].astype(F32)
    core = core_index()
    above, below = rim_masks(core)
    own_first = jnp.zeros((8, LANES), jnp.int32) + core == 0
    low = lax.broadcasted_iota(jnp.int32, (8, LANES), 1) < LANES // 2

    def work(group, carry):
        march = March(field, group)

        def column(place, rate, blocks, rim):
            place = pl.multiple_of(place, 8)
            row = pl.multiple_of(8 + place, 8)
            state = march.fresh()
            march.layer(row, 0, rate, state, before=before_wide.at[pl.ds(place, 8)], rim=rim)
            for t in range(TILES):
                for block in blocks(t):
                    for k in range(4):
                        state["color"][k][t] = state["color"][k][t] + state["reach"][t] * block[k + 1]
                    state["path"][t] = state["path"][t] + block[0]
                    state["reach"][t] = jnp.exp2(state["path"][t])
            march.layer(row, layers - 1, rate, state, after=after_wide.at[pl.ds(place, 8)], rim=rim)
            side = rate[1][...]
            for t in range(TILES):
                path = state["path"][t]
                red, green, blue, total = (kind[t] for kind in state["color"])
                factor = jnp.where(side > 0, jnp.exp2(-path), -1.0) * TONE
                final = [(red - 0.8 * total) * factor, green * factor, (1.2 * total - blue) * factor, jnp.abs(path)]
                for k in range(4):
                    levels[k, t, pl.ds(place, 8), :] = encode(final[k])

        def outside(t):
            return [[border[k, :, march.here(t)] for k in range(5)]]

        def inside(t):
            mine = [own[k, :, march.here(t)] for k in range(5)]
            others = [other[k, :, march.here(t)] for k in range(5)]
            return (
                [jnp.where(own_first, a, b) for a, b in zip(mine, others)],
                [jnp.where(own_first, b, a) for a, b in zip(mine, others)],
            )

        column(8 * core, rates_of(rates, 24 * core), outside, (beyond_wide, above, below))
        column(8 - 8 * core, rates_of(rates, 8 + 8 * core), inside, None)
        for t in range(TILES):
            z = march.tile(t)
            even, odd = [], []
            for k in range(4):
                top, bottom = levels[k, t, pl.ds(0, 8)], levels[k, t, pl.ds(8, 8)]
                even.append(jnp.where(low, top, pltpu.roll(bottom, LANES // 2, 1)))
                odd.append(jnp.where(low, pltpu.roll(top, LANES // 2, 1), bottom))
            for k in range(2):
                codes[2 * z, k] = jnp.concatenate(even[2 * k : 2 * k + 2], 0).astype(jnp.int16)
                codes[2 * z + 1, k] = jnp.concatenate(odd[2 * k : 2 * k + 2], 0).astype(jnp.int16)
        return carry

    lax.fori_loop(0, tiles // TILES, work, 0)


def fold_kernel(codes, view, out):
    bricks = codes.shape[0]
    column = side_column(view)
    low = lax.broadcasted_iota(jnp.int32, (8, LANES), 1) < LANES // 2
    for core in range(2):
        base = 16 * core
        side = jnp.where(low, column[base : base + 8], column[base + 8 : base + 16])
        backward = side > 0
        path = jnp.zeros((8, LANES), F32)
        color = [jnp.zeros((8, LANES), F32) for _ in range(3)]
        for k in range(core, bricks, 2):
            values = [decode(codes[k, 0]), decode(codes[k, 1])]
            farther = path + values[1][8:]
            reach = jnp.exp2(side * jnp.where(backward, farther, path))
            path = farther
            color[0] = color[0] + reach * values[0][:8]
            color[1] = color[1] + reach * values[0][8:]
            color[2] = color[2] + reach * values[1][:8]
        passing = jnp.exp2(-path)
        factor = jnp.where(backward, passing, 1.0)
        parts = [c * factor for c in color] + [1.0 - passing]
        for q in range(4):
            out[q, pl.ds(base, 8), :] = parts[q][:, : LANES // 2]
            out[q, pl.ds(base + 8, 8), :] = parts[q][:, LANES // 2 :]


def body(volume, view_side):
    layers, rows, depth = volume.shape
    size_x, size_y = lax.axis_size("bx"), lax.axis_size("by")
    half = rows // 2
    mates = [(i, i ^ 1) for i in range(size_x)]
    up_x = [(i, i + 2) for i in range(size_x - 2)]
    down_x = [(j, i) for i, j in up_x]
    across = []
    for i in range(0, size_x, 2):
        for j in range(size_y - 1):
            upper, lower = (i + 1) * size_y + j, i * size_y + j + 1
            across += [(upper, lower), (lower, upper)]
    view = view_side[None, :]
    in_vmem = pl.BlockSpec(memory_space=pltpu.VMEM)
    shape = jax.ShapeDtypeStruct

    def call(kernel, operands, out_shape, scratch, name, cost=0, limit=24, aliases={}):
        return pl.pallas_call(
            kernel,
            out_shape=out_shape,
            in_specs=[in_vmem] * len(operands),
            out_specs=jax.tree.map(lambda _: in_vmem, out_shape),
            scratch_shapes=scratch,
            input_output_aliases=aliases,
            compiler_params=pltpu.CompilerParams(vmem_limit_bytes=limit << 20),
            cost_estimate=pl.CostEstimate(flops=cost, bytes_accessed=2 * layers * rows * depth, transcendentals=0) if cost else None,
            name=name,
        )(*operands)

    work = 40 * layers * half * depth
    face, part = shape((half, depth), BF16), shape((5, 8, depth), F32)
    brick = shape((2 * layers, depth // LANES + 2, half + 16, LANES), F32)
    send = call(share_kernel, (volume,), shape((layers + 1, half, depth), BF16), [], "share")
    mate = lax.ppermute(send, "bx", mates)
    own, field, rates, own_end, own_rim = call(
        functools.partial(own_kernel, layers * size_x),
        (volume, view),
        (part, brick, shape((2, rows, LANES), F32), face, face),
        [],
        "own",
        work // 2,
    )
    first, last, rim = call(face_kernel, (mate, own_end, own_rim), (face, face, shape((2 * layers, depth), BF16)), [], "face")
    beyond = lax.ppermute(rim, ("bx", "by"), across)
    before = lax.ppermute(last, "bx", up_x)
    after = lax.ppermute(first, "bx", down_x)
    other, field = call(mate_kernel, (mate, rates, field), (part, brick), [], "mate", work // 2, aliases={2: 1})
    wide, rim_wide = pltpu.VMEM((half, depth), F32), pltpu.VMEM((2 * layers, depth), F32)
    border = call(rim_kernel, (beyond, rates, field), part, [rim_wide], "rim", work)
    codes = call(
        outer_kernel,
        (before, after, beyond, rates, own, other, border, field),
        shape((size_x, 2, 16, LANES), jnp.int16),
        [wide, wide, rim_wide, pltpu.VMEM((4, TILES, 16, LANES), jnp.int32)],
        "outer",
        work,
    )
    codes = lax.all_to_all(codes, "bx", split_axis=0, concat_axis=0, tiled=True)
    return call(fold_kernel, (codes, view), shape((4, rows, depth // size_x), F32), [], "fold")


def solution(mesh):
    placed = (P("bx", "by", None), P("by"))
    return jax.shard_map(body, mesh=mesh, in_specs=placed, out_specs=P(None, "by", "bx"), check_vma=False)
```

```python
import functools
import math

import jax
import jax.numpy as jnp
from jax import lax
from jax.experimental import pallas as pl
from jax.experimental.pallas import tpu as pltpu
from jax.sharding import PartitionSpec as P

F32 = jnp.float32
BF16 = jnp.bfloat16
LANES = 128
TILES = 8
LOG2E = 1.0 / math.log(2.0)
FLOOR = -27.0
STEPS = 2570.0
TONE = 0.7 * 0.48 * 0.48


def recip(x):
    return pl.reciprocal(x, approx=True)


def lane_tile(start):
    return pl.ds(pl.multiple_of(start, LANES), LANES)


def encode(value):
    level = jnp.log2(jnp.maximum(value, 2.0**FLOOR)) * STEPS + (0.5 - FLOOR * STEPS)
    return level.astype(jnp.int32) - 32768


def decode(code):
    code = code.astype(jnp.int32)
    value = jnp.exp2(code.astype(F32) * (1.0 / STEPS) + (32768.0 / STEPS + FLOOR))
    return jnp.where(code == -32768, 0.0, value)


def core_index():
    return lax.rem(lax.axis_index("bx"), 2)


def side_column(view):
    rows = view.shape[1]
    spread = jnp.broadcast_to(view[...].astype(F32), (rows, rows))
    down = lax.broadcasted_iota(jnp.int32, (rows, rows), 0)
    along = lax.broadcasted_iota(jnp.int32, (rows, rows), 1)
    picked = jnp.sum(jnp.where(down == along, spread, 0.0), axis=1, keepdims=True)
    return jnp.where(picked > 0.5, 1.0, -1.0)


def one_row(ref, row, here):
    return jnp.concatenate([ref[l, :, here].astype(F32)[row : row + 1] for l in range(16)], 0).astype(BF16)


def end_kernel(vol, end):
    depth = vol.shape[2]
    layer = (vol.shape[0] - 1) * core_index()

    def tile(z, carry):
        here = lane_tile(LANES * z)
        end[:, here] = vol[layer, :, here]
        return carry

    lax.fori_loop(0, depth // LANES, tile, 0, unroll=8)


def share_kernel(vol, end, send):
    layers, rows, depth = vol.shape
    half = rows // 2

    def share(far, row):
        def tile(z, carry):
            here = lane_tile(LANES * z)
            for l in range(layers):
                send[l, :, here] = vol[l, pl.ds(far, half), here]
            send[layers, :, here] = one_row(vol, row, here)
            return carry

        lax.fori_loop(0, depth // LANES, tile, 0, unroll=2)

    core = core_index()

    @pl.when(core == 0)
    def _():
        share(half, half - 1)

    @pl.when(core == 1)
    def _():
        share(0, half)


def own_edge(vol, core, rim):
    rows, depth = vol.shape[1], vol.shape[2]

    def edge(row):
        def tile(z, carry):
            here = lane_tile(LANES * z)
            rim[:, here] = one_row(vol, row, here)
            return carry

        lax.fori_loop(0, depth // LANES, tile, 0, unroll=2)

    @pl.when(core == 0)
    def _():
        edge(0)

    @pl.when(core == 1)
    def _():
        edge(rows - 1)


def rim_rows_kernel(mate, own_rim, rim):
    layers, half, depth = mate.shape[0] - 1, mate.shape[1], mate.shape[2]

    def edge(own_at, mate_at, row):
        def tile(z, carry):
            here = lane_tile(LANES * z)
            rim[pl.ds(own_at, layers), here] = own_rim[:, here]
            rim[pl.ds(mate_at, layers), here] = one_row(mate, row, here)
            return carry

        lax.fori_loop(0, depth // LANES, tile, 0, unroll=4)

    core = core_index()

    @pl.when(core == 0)
    def _():
        edge(0, layers, 0)

    @pl.when(core == 1)
    def _():
        edge(layers, 0, half - 1)


def hand_kernel(face, rim, hand_on):
    half, depth = hand_on.shape
    far = pl.multiple_of(half - half * core_index(), half)

    def tile(z, carry):
        here = lane_tile(LANES * z)
        hand_on[:, here] = face[pl.ds(far, half), here]
        return carry

    lax.fori_loop(0, depth // LANES, tile, 0, unroll=8)


class March:
    def __init__(self, field, group):
        self.field, self.group = field, group
        self.lane = lax.broadcasted_iota(jnp.int32, (8, LANES), 1)

    def tile(self, t):
        return self.group * TILES + t

    def here(self, t):
        return lane_tile(LANES * self.tile(t))

    def at(self, l, t, row):
        return self.field[l, self.tile(t) + 1, pl.ds(row, 8), :]

    def fresh(self):
        return dict(
            path=[jnp.zeros((8, LANES), F32) for _ in range(TILES)],
            reach=[jnp.ones((8, LANES), F32) for _ in range(TILES)],
            color=[[jnp.zeros((8, LANES), F32) for _ in range(TILES)] for _ in range(4)],
        )

    def layer(self, row, l, rate, state, before=None, after=None, rim=None):
        lane = self.lane
        path, reach, color = state["path"], state["reach"], state["color"]
        mid = [self.at(l, t, row) for t in range(-1, TILES + 1)]
        from_left = [pltpu.roll(v, 1, 1) for v in mid[:-1]]
        from_right = [pltpu.roll(v, LANES - 1, 1) for v in mid[1:]]
        for t in range(TILES):
            v = mid[t + 1]
            up, down = self.at(l, t, row - 1), self.at(l, t, row + 1)
            if rim is not None:
                beyond = jnp.broadcast_to(rim[0][pl.ds(l, 1), self.here(t)], (8, LANES))
                up, down = jnp.where(rim[1], beyond, up), jnp.where(rim[2], beyond, down)
            back = self.at(l - 1, t, row) if before is None else before[:, self.here(t)]
            front = self.at(l + 1, t, row) if after is None else after[:, self.here(t)]
            gx = front - back
            gy = down - up
            gz = jnp.where(lane == LANES - 1, from_right[t + 1], from_right[t]) - jnp.where(
                lane == 0, from_left[t], from_left[t + 1]
            )
            square = gx * gx + gy * gy + gz * gz
            facing = gx + (0.6 / 0.48) * gy + (0.64 / 0.48) * gz
            shading = 0.3 / TONE + facing * facing * recip(square + 4.0)
            lifted = jnp.maximum(v, 0.4)
            density = jnp.minimum(lifted, 1.6) - 0.4
            path[t] = path[t] + density * (rate[0][...] - rate[1][...] * recip(square + 1.0))
            next_reach = jnp.exp2(path[t])
            weight = (next_reach - reach[t]) * shading
            reach[t] = next_reach
            color[0][t] = color[0][t] + weight * jnp.clip(v, 0.8, 1.8)
            color[1][t] = color[1][t] + weight * jnp.minimum(v, 2.0 - v)
            color[2][t] = color[2][t] + weight * jnp.minimum(lifted, 1.2)
            color[3][t] = color[3][t] + weight

    def keep(self, state, part):
        for t in range(TILES):
            for k, kind in enumerate([state["path"]] + state["color"]):
                part[k, :, self.here(t)] = kind[t]


def set_rates(view, ray_length, rates):
    rows = rates.shape[1]
    side = jnp.broadcast_to(side_column(view), (rows, LANES))
    scale = 3.0 / 1.2 / ray_length * LOG2E
    rates[0] = side * (1.25 * scale)
    rates[1] = side * scale


def rates_of(rates, row):
    here = pl.ds(pl.multiple_of(row, 8), 8)
    return rates.at[0, here], rates.at[1, here]


def own_kernel(ray_length, vol, view, part, field, rates, rim):
    layers, rows, depth = vol.shape
    tiles, half = depth // LANES, rows // 2
    set_rates(view, ray_length, rates)
    core = core_index()
    own_edge(vol, core, rim)
    mine = layers * core

    def widen(first, beside):
        def one(l, carry):
            field[mine + l, 0] = jnp.zeros((rows, LANES), F32)
            field[mine + l, tiles + 1] = jnp.zeros((rows, LANES), F32)
            for tile in range(tiles):
                here = pl.ds(LANES * tile, LANES)
                field[mine + l, tile + 1, pl.ds(8, half), :] = vol[l, pl.ds(first, half), here].astype(F32)
                near = vol[l, pl.ds(half - first, half), here].astype(F32)
                field[mine + l, tile + 1, pl.ds(beside[1], 8), :] = near[beside[0] : beside[0] + 8]
            return carry

        lax.fori_loop(0, layers, one, 0)

    @pl.when(core == 0)
    def _():
        widen(0, (0, half + 8))

    @pl.when(core == 1)
    def _():
        widen(half, (half - 8, 0))

    row = pl.multiple_of(16 - 8 * core, 8)

    def work(group, carry):
        march = March(field, group)
        state = march.fresh()
        for l in range(1, layers - 1):
            march.layer(row, mine + l, rates_of(rates, 8 + 8 * core), state)
        march.keep(state, part)
        return carry

    lax.fori_loop(0, tiles // TILES, work, 0)


def mate_kernel(mate, rates, own_field, part, field):
    layers, half, depth = mate.shape[0] - 1, mate.shape[1], mate.shape[2]
    tiles = depth // LANES
    core = core_index()
    inside = pl.ds(8, half)
    other = layers * (1 - core)

    def widen(l, carry):
        field[other + l, 0, inside, :] = jnp.zeros((half, LANES), F32)
        field[other + l, tiles + 1, inside, :] = jnp.zeros((half, LANES), F32)
        for tile in range(tiles):
            field[other + l, tile + 1, inside, :] = mate[l, :, pl.ds(LANES * tile, LANES)].astype(F32)
        return carry

    lax.fori_loop(0, layers, widen, 0)

    def border(slot, other):
        def tile(z, carry):
            field[pl.ds(other, layers), z + 1, slot, :] = mate[layers, :, lane_tile(LANES * z)].astype(F32)
            return carry

        lax.fori_loop(0, tiles, tile, 0, unroll=2)

    @pl.when(core == 0)
    def _():
        border(half + 8, layers)

    @pl.when(core == 1)
    def _():
        border(7, 0)

    row = pl.multiple_of(16 - 8 * core, 8)
    begin = layers - 1 - (layers - 2) * core

    def work(group, carry):
        march = March(field, group)
        state = march.fresh()
        for k in range(layers):
            march.layer(row, begin + k, rates_of(rates, 8 + 8 * core), state)
        march.keep(state, part)
        return carry

    lax.fori_loop(0, tiles // TILES, work, 0)


def rim_masks(core):
    rows_down = lax.broadcasted_iota(jnp.int32, (8, LANES), 0)
    return rows_down == 8 * core, rows_down == 8 - core


def rim_kernel(beyond, rates, field, part, beyond_wide):
    layers = field.shape[0]
    tiles = part.shape[2] // LANES
    beyond_wide[...] = beyond[...].astype(F32)
    core = core_index()
    above, below = rim_masks(core)
    row = pl.multiple_of(8 + 8 * core, 8)

    def work(group, carry):
        march = March(field, group)
        state = march.fresh()
        for l in range(1, layers - 1):
            march.layer(row, l, rates_of(rates, 24 * core), state, rim=(beyond_wide, above, below))
        march.keep(state, part)
        return carry

    lax.fori_loop(0, tiles // TILES, work, 0)


def outer_kernel(face, handed, beyond, rates, own, other, border, field, codes, before_wide, after_wide, beyond_wide, levels):
    layers = field.shape[0]
    tiles = own.shape[2] // LANES
    beyond_wide[...] = beyond[...].astype(F32)
    core = core_index()
    half = before_wide.shape[0]

    @pl.when(core == 0)
    def _():
        before_wide[...] = face[pl.ds(0, half)].astype(F32)
        after_wide[...] = handed[...].astype(F32)

    @pl.when(core == 1)
    def _():
        before_wide[...] = handed[...].astype(F32)
        after_wide[...] = face[pl.ds(half, half)].astype(F32)

    above, below = rim_masks(core)
    own_first = jnp.zeros((8, LANES), jnp.int32) + core == 0
    low = lax.broadcasted_iota(jnp.int32, (8, LANES), 1) < LANES // 2

    def work(group, carry):
        march = March(field, group)

        def column(place, rate, blocks, rim):
            place = pl.multiple_of(place, 8)
            row = pl.multiple_of(8 + place, 8)
            state = march.fresh()
            march.layer(row, 0, rate, state, before=before_wide.at[pl.ds(place, 8)], rim=rim)
            for t in range(TILES):
                for block in blocks(t):
                    for k in range(4):
                        state["color"][k][t] = state["color"][k][t] + state["reach"][t] * block[k + 1]
                    state["path"][t] = state["path"][t] + block[0]
                    state["reach"][t] = jnp.exp2(state["path"][t])
            march.layer(row, layers - 1, rate, state, after=after_wide.at[pl.ds(place, 8)], rim=rim)
            side = rate[1][...]
            for t in range(TILES):
                path = state["path"][t]
                red, green, blue, total = (kind[t] for kind in state["color"])
                factor = jnp.where(side > 0, jnp.exp2(-path), -1.0) * TONE
                final = [(red - 0.8 * total) * factor, green * factor, (1.2 * total - blue) * factor, jnp.abs(path)]
                for k in range(4):
                    levels[k, t, pl.ds(place, 8), :] = encode(final[k])

        def outside(t):
            return [[border[k, :, march.here(t)] for k in range(5)]]

        def inside(t):
            mine = [own[k, :, march.here(t)] for k in range(5)]
            others = [other[k, :, march.here(t)] for k in range(5)]
            return (
                [jnp.where(own_first, a, b) for a, b in zip(mine, others)],
                [jnp.where(own_first, b, a) for a, b in zip(mine, others)],
            )

        column(8 * core, rates_of(rates, 24 * core), outside, (beyond_wide, above, below))
        column(8 - 8 * core, rates_of(rates, 8 + 8 * core), inside, None)
        for t in range(TILES):
            z = march.tile(t)
            even, odd = [], []
            for k in range(4):
                top, bottom = levels[k, t, pl.ds(0, 8)], levels[k, t, pl.ds(8, 8)]
                even.append(jnp.where(low, top, pltpu.roll(bottom, LANES // 2, 1)))
                odd.append(jnp.where(low, pltpu.roll(top, LANES // 2, 1), bottom))
            for k in range(2):
                codes[2 * z, k] = jnp.concatenate(even[2 * k : 2 * k + 2], 0).astype(jnp.int16)
                codes[2 * z + 1, k] = jnp.concatenate(odd[2 * k : 2 * k + 2], 0).astype(jnp.int16)
        return carry

    lax.fori_loop(0, tiles // TILES, work, 0)


def fold_kernel(codes, view, out):
    bricks = codes.shape[0]
    column = side_column(view)
    low = lax.broadcasted_iota(jnp.int32, (8, LANES), 1) < LANES // 2
    for core in range(2):
        base = 16 * core
        side = jnp.where(low, column[base : base + 8], column[base + 8 : base + 16])
        backward = side > 0
        path = jnp.zeros((8, LANES), F32)
        color = [jnp.zeros((8, LANES), F32) for _ in range(3)]
        for k in range(core, bricks, 2):
            values = [decode(codes[k, 0]), decode(codes[k, 1])]
            farther = path + values[1][8:]
            reach = jnp.exp2(side * jnp.where(backward, farther, path))
            path = farther
            color[0] = color[0] + reach * values[0][:8]
            color[1] = color[1] + reach * values[0][8:]
            color[2] = color[2] + reach * values[1][:8]
        passing = jnp.exp2(-path)
        factor = jnp.where(backward, passing, 1.0)
        parts = [c * factor for c in color] + [1.0 - passing]
        for q in range(4):
            out[q, pl.ds(base, 8), :] = parts[q][:, : LANES // 2]
            out[q, pl.ds(base + 8, 8), :] = parts[q][:, LANES // 2 :]


def body(volume, view_side):
    layers, rows, depth = volume.shape
    size_x, size_y = lax.axis_size("bx"), lax.axis_size("by")
    half = rows // 2
    mates = [(i, i ^ 1) for i in range(size_x)]
    chips = [(i, i + 1) for i in range(1, size_x - 1, 2)]
    chips += [(j, i) for i, j in chips]
    across = []
    for i in range(0, size_x, 2):
        for j in range(size_y - 1):
            upper, lower = (i + 1) * size_y + j, i * size_y + j + 1
            across += [(upper, lower), (lower, upper)]
    view = view_side[None, :]
    in_vmem = pl.BlockSpec(memory_space=pltpu.VMEM)
    shape = jax.ShapeDtypeStruct

    def call(kernel, operands, out_shape, scratch, name, cost=0, limit=24, aliases={}):
        return pl.pallas_call(
            kernel,
            out_shape=out_shape,
            in_specs=[in_vmem] * len(operands),
            out_specs=jax.tree.map(lambda _: in_vmem, out_shape),
            scratch_shapes=scratch,
            input_output_aliases=aliases,
            compiler_params=pltpu.CompilerParams(vmem_limit_bytes=limit << 20),
            cost_estimate=pl.CostEstimate(flops=cost, bytes_accessed=2 * layers * rows * depth, transcendentals=0) if cost else None,
            name=name,
        )(*operands)

    work = 40 * layers * half * depth
    face, part = shape((half, depth), BF16), shape((5, 8, depth), F32)
    brick = shape((2 * layers, depth // LANES + 2, half + 16, LANES), F32)
    end = call(end_kernel, (volume,), shape((rows, depth), BF16), [], "end")
    end_in = lax.ppermute(end, "bx", chips)
    send = call(share_kernel, (volume, end), shape((layers + 1, half, depth), BF16), [], "share")
    mate = lax.ppermute(send, "bx", mates)
    own, field, rates, own_rim = call(
        functools.partial(own_kernel, layers * size_x),
        (volume, view),
        (part, brick, shape((2, rows, LANES), F32), face),
        [],
        "own",
        work // 2,
    )
    rim = call(rim_rows_kernel, (mate, own_rim), shape((2 * layers, depth), BF16), [], "rim_rows")
    beyond = lax.ppermute(rim, ("bx", "by"), across)
    hand_on = call(hand_kernel, (end_in, rim), face, [], "hand")
    handed = lax.ppermute(hand_on, "bx", mates)
    other, field = call(mate_kernel, (mate, rates, field), (part, brick), [], "mate", work // 2, aliases={2: 1})
    wide, rim_wide = pltpu.VMEM((half, depth), F32), pltpu.VMEM((2 * layers, depth), F32)
    border = call(rim_kernel, (beyond, rates, field), part, [rim_wide], "rim", work)
    codes = call(
        outer_kernel,
        (end_in, handed, beyond, rates, own, other, border, field),
        shape((size_x, 2, 16, LANES), jnp.int16),
        [wide, wide, rim_wide, pltpu.VMEM((4, TILES, 16, LANES), jnp.int32)],
        "outer",
        work,
    )
    codes = lax.all_to_all(codes, "bx", split_axis=0, concat_axis=0, tiled=True)
    return call(fold_kernel, (codes, view), shape((4, rows, depth // size_x), F32), [], "fold")


def solution(mesh):
    placed = (P("bx", "by", None), P("by"))
    return jax.shard_map(body, mesh=mesh, in_specs=placed, out_specs=P(None, "by", "bx"), check_vma=False)
```

```python
import functools
import math

import jax
import jax.numpy as jnp
from jax import lax
from jax.experimental import pallas as pl
from jax.experimental.pallas import tpu as pltpu
from jax.sharding import PartitionSpec as P

F32 = jnp.float32
BF16 = jnp.bfloat16
LANES = 128
TILES = 16
LOG2E = 1.0 / math.log(2.0)
FLOOR = -27.0
STEPS = 2570.0
TONE = 0.7 * 0.48 * 0.48
FOOT = 0.4


def recip(x):
    return pl.reciprocal(x, approx=True)


def lane_tile(start):
    return pl.ds(pl.multiple_of(start, LANES), LANES)


def encode(value):
    level = jnp.log2(jnp.maximum(value, 2.0**FLOOR)) * STEPS + (0.5 - FLOOR * STEPS)
    return level.astype(jnp.int32) - 32768


def decode(code):
    code = code.astype(jnp.int32)
    value = jnp.exp2(code.astype(F32) * (1.0 / STEPS) + (32768.0 / STEPS + FLOOR))
    return jnp.where(code == -32768, 0.0, value)


def lower(stored):
    return stored.astype(F32) - FOOT


def core_index():
    return lax.rem(lax.axis_index("bx"), 2)


def side_column(view):
    rows = view.shape[1]
    spread = jnp.broadcast_to(view[...].astype(F32), (rows, rows))
    down = lax.broadcasted_iota(jnp.int32, (rows, rows), 0)
    along = lax.broadcasted_iota(jnp.int32, (rows, rows), 1)
    picked = jnp.sum(jnp.where(down == along, spread, 0.0), axis=1, keepdims=True)
    return jnp.where(picked > 0.5, 1.0, -1.0)


def one_row(ref, row, here):
    return jnp.concatenate([ref[l, :, here].astype(F32)[row : row + 1] for l in range(16)], 0).astype(BF16)


def share_kernel(vol, send, end):
    layers, rows, depth = vol.shape
    half = rows // 2

    def share(far, row, face):
        def tile(z, carry):
            here = lane_tile(LANES * z)
            for l in range(layers):
                send[l, :, here] = vol[l, pl.ds(far, half), here]
            send[layers, :, here] = one_row(vol, row, here)
            end[:, here] = vol[face, :, here]
            return carry

        lax.fori_loop(0, depth // LANES, tile, 0, unroll=2)

    core = core_index()

    @pl.when(core == 0)
    def _():
        share(half, half - 1, 0)

    @pl.when(core == 1)
    def _():
        share(0, half, layers - 1)


def own_edge(vol, core, rim):
    rows, depth = vol.shape[1], vol.shape[2]

    def edge(row):
        def tile(z, carry):
            here = lane_tile(LANES * z)
            rim[:, here] = one_row(vol, row, here)
            return carry

        lax.fori_loop(0, depth // LANES, tile, 0, unroll=2)

    @pl.when(core == 0)
    def _():
        edge(0)

    @pl.when(core == 1)
    def _():
        edge(rows - 1)


def rim_rows_kernel(mate, own_rim, rim):
    layers, half, depth = mate.shape[0] - 1, mate.shape[1], mate.shape[2]

    def edge(own_at, mate_at, row):
        def tile(z, carry):
            here = lane_tile(LANES * z)
            rim[pl.ds(own_at, layers), here] = own_rim[:, here]
            rim[pl.ds(mate_at, layers), here] = one_row(mate, row, here)
            return carry

        lax.fori_loop(0, depth // LANES, tile, 0, unroll=4)

    core = core_index()

    @pl.when(core == 0)
    def _():
        edge(0, layers, 0)

    @pl.when(core == 1)
    def _():
        edge(layers, 0, half - 1)


def hand_kernel(face, rim, hand_on):
    half, depth = hand_on.shape
    far = pl.multiple_of(half - half * core_index(), half)

    def tile(z, carry):
        here = lane_tile(LANES * z)
        hand_on[:, here] = face[pl.ds(far, half), here]
        return carry

    lax.fori_loop(0, depth // LANES, tile, 0, unroll=8)


class March:
    def __init__(self, field, group):
        self.field, self.group = field, group
        self.lane = lax.broadcasted_iota(jnp.int32, (8, LANES), 1)

    def tile(self, t):
        return self.group * TILES + t

    def here(self, t):
        return lane_tile(LANES * self.tile(t))

    def at(self, l, t, row):
        return self.field[l, self.tile(t) + 1, pl.ds(row, 8), :]

    def fresh(self):
        return dict(
            path=[jnp.zeros((8, LANES), F32) for _ in range(TILES)],
            reach=[jnp.ones((8, LANES), F32) for _ in range(TILES)],
            color=[[jnp.zeros((8, LANES), F32) for _ in range(TILES)] for _ in range(4)],
        )

    def layer(self, row, l, rate, state, before=None, after=None, rim=None):
        lane = self.lane
        path, reach, color = state["path"], state["reach"], state["color"]
        mid = [self.at(l, t, row) for t in range(-1, TILES + 1)]
        from_left = [pltpu.roll(v, 1, 1) for v in mid[:-1]]
        from_right = [pltpu.roll(v, LANES - 1, 1) for v in mid[1:]]
        for t in range(TILES):
            v = mid[t + 1]
            up, down = self.at(l, t, row - 1), self.at(l, t, row + 1)
            if rim is not None:
                beyond = jnp.broadcast_to(rim[0][pl.ds(l, 1), self.here(t)], (8, LANES))
                up, down = jnp.where(rim[1], beyond, up), jnp.where(rim[2], beyond, down)
            back = self.at(l - 1, t, row) if before is None else before[:, self.here(t)]
            front = self.at(l + 1, t, row) if after is None else after[:, self.here(t)]
            gx = front - back
            gy = down - up
            gz = jnp.where(lane == LANES - 1, from_right[t + 1], from_right[t]) - jnp.where(
                lane == 0, from_left[t], from_left[t + 1]
            )
            square = gx * gx + gy * gy + gz * gz
            facing = gx + (0.6 / 0.48) * gy + (0.64 / 0.48) * gz
            shading = 0.3 / TONE + facing * facing * recip(square + 4.0)
            lifted = jnp.maximum(v, 0.0)
            density = jnp.minimum(lifted, 1.2)
            path[t] = path[t] + density * (rate[0][...] - rate[1][...] * recip(square + 1.0))
            next_reach = jnp.exp2(path[t])
            weight = (next_reach - reach[t]) * shading
            reach[t] = next_reach
            color[0][t] = color[0][t] + weight * jnp.clip(v, 0.8 - FOOT, 1.8 - FOOT)
            color[1][t] = color[1][t] + weight * jnp.minimum(v, 2.0 - 2.0 * FOOT - v)
            color[2][t] = color[2][t] + weight * jnp.minimum(lifted, 1.2 - FOOT)
            color[3][t] = color[3][t] + weight

    def keep(self, state, part):
        for t in range(TILES):
            for k, kind in enumerate([state["path"]] + state["color"]):
                part[k, :, self.here(t)] = kind[t]


def set_rates(view, ray_length, rates):
    rows = rates.shape[1]
    side = jnp.broadcast_to(side_column(view), (rows, LANES))
    scale = 3.0 / 1.2 / ray_length * LOG2E
    rates[0] = side * (1.25 * scale)
    rates[1] = side * scale


def rates_of(rates, row):
    here = pl.ds(pl.multiple_of(row, 8), 8)
    return rates.at[0, here], rates.at[1, here]


def own_kernel(ray_length, vol, view, part, field, rates, rim):
    layers, rows, depth = vol.shape
    tiles, half = depth // LANES, rows // 2
    set_rates(view, ray_length, rates)
    core = core_index()
    own_edge(vol, core, rim)
    mine = layers * core

    def widen(first, beside):
        def one(l, carry):
            field[mine + l, 0] = jnp.full((rows, LANES), -FOOT, F32)
            field[mine + l, tiles + 1] = jnp.full((rows, LANES), -FOOT, F32)
            for tile in range(tiles):
                here = pl.ds(LANES * tile, LANES)
                field[mine + l, tile + 1, pl.ds(8, half), :] = lower(vol[l, pl.ds(first, half), here])
                near = lower(vol[l, pl.ds(half - first, half), here])
                field[mine + l, tile + 1, pl.ds(beside[1], 8), :] = near[beside[0] : beside[0] + 8]
            return carry

        lax.fori_loop(0, layers, one, 0)

    @pl.when(core == 0)
    def _():
        widen(0, (0, half + 8))

    @pl.when(core == 1)
    def _():
        widen(half, (half - 8, 0))

    row = pl.multiple_of(16 - 8 * core, 8)

    def work(group, carry):
        march = March(field, group)
        state = march.fresh()
        for l in range(1, layers - 1):
            march.layer(row, mine + l, rates_of(rates, 8 + 8 * core), state)
        march.keep(state, part)
        return carry

    lax.fori_loop(0, tiles // TILES, work, 0)


def mate_kernel(mate, rates, own_field, part, field):
    layers, half, depth = mate.shape[0] - 1, mate.shape[1], mate.shape[2]
    tiles = depth // LANES
    core = core_index()
    inside = pl.ds(8, half)
    other = layers * (1 - core)

    def widen(l, carry):
        field[other + l, 0, inside, :] = jnp.full((half, LANES), -FOOT, F32)
        field[other + l, tiles + 1, inside, :] = jnp.full((half, LANES), -FOOT, F32)
        for tile in range(tiles):
            field[other + l, tile + 1, inside, :] = lower(mate[l, :, pl.ds(LANES * tile, LANES)])
        return carry

    lax.fori_loop(0, layers, widen, 0)

    def border(slot, other):
        def tile(z, carry):
            field[pl.ds(other, layers), z + 1, slot, :] = lower(mate[layers, :, lane_tile(LANES * z)])
            return carry

        lax.fori_loop(0, tiles, tile, 0, unroll=2)

    @pl.when(core == 0)
    def _():
        border(half + 8, layers)

    @pl.when(core == 1)
    def _():
        border(7, 0)

    row = pl.multiple_of(16 - 8 * core, 8)
    begin = layers - 1 - (layers - 2) * core

    def work(group, carry):
        march = March(field, group)
        state = march.fresh()
        for k in range(layers):
            march.layer(row, begin + k, rates_of(rates, 8 + 8 * core), state)
        march.keep(state, part)
        return carry

    lax.fori_loop(0, tiles // TILES, work, 0)


def rim_masks(core):
    rows_down = lax.broadcasted_iota(jnp.int32, (8, LANES), 0)
    return rows_down == 8 * core, rows_down == 8 - core


def rim_kernel(beyond, rates, field, part, beyond_wide):
    layers = field.shape[0]
    tiles = part.shape[2] // LANES
    beyond_wide[...] = lower(beyond[...])
    core = core_index()
    above, below = rim_masks(core)
    row = pl.multiple_of(8 + 8 * core, 8)

    def work(group, carry):
        march = March(field, group)
        state = march.fresh()
        for l in range(1, layers - 1):
            march.layer(row, l, rates_of(rates, 24 * core), state, rim=(beyond_wide, above, below))
        march.keep(state, part)
        return carry

    lax.fori_loop(0, tiles // TILES, work, 0)


def outer_kernel(face, handed, beyond, rates, own, other, border, field, codes, before_wide, after_wide, beyond_wide, levels):
    layers = field.shape[0]
    tiles = own.shape[2] // LANES
    beyond_wide[...] = lower(beyond[...])
    core = core_index()
    half = before_wide.shape[0]

    @pl.when(core == 0)
    def _():
        before_wide[...] = lower(face[pl.ds(0, half)])
        after_wide[...] = lower(handed[...])

    @pl.when(core == 1)
    def _():
        before_wide[...] = lower(handed[...])
        after_wide[...] = lower(face[pl.ds(half, half)])

    above, below = rim_masks(core)
    own_first = jnp.zeros((8, LANES), jnp.int32) + core == 0
    low = lax.broadcasted_iota(jnp.int32, (8, LANES), 1) < LANES // 2

    def work(group, carry):
        march = March(field, group)

        def column(place, rate, blocks, rim):
            place = pl.multiple_of(place, 8)
            row = pl.multiple_of(8 + place, 8)
            state = march.fresh()
            march.layer(row, 0, rate, state, before=before_wide.at[pl.ds(place, 8)], rim=rim)
            for t in range(TILES):
                for block in blocks(t):
                    for k in range(4):
                        state["color"][k][t] = state["color"][k][t] + state["reach"][t] * block[k + 1]
                    state["path"][t] = state["path"][t] + block[0]
                    state["reach"][t] = jnp.exp2(state["path"][t])
            march.layer(row, layers - 1, rate, state, after=after_wide.at[pl.ds(place, 8)], rim=rim)
            side = rate[1][...]
            for t in range(TILES):
                path = state["path"][t]
                red, green, blue, total = (kind[t] for kind in state["color"])
                factor = jnp.where(side > 0, jnp.exp2(-path), -1.0) * TONE
                final = [(red - (0.8 - FOOT) * total) * factor, (green + FOOT * total) * factor, ((1.2 - FOOT) * total - blue) * factor, jnp.abs(path)]
                for k in range(4):
                    levels[k, t, pl.ds(place, 8), :] = encode(final[k])

        def outside(t):
            return [[border[k, :, march.here(t)] for k in range(5)]]

        def inside(t):
            mine = [own[k, :, march.here(t)] for k in range(5)]
            others = [other[k, :, march.here(t)] for k in range(5)]
            return (
                [jnp.where(own_first, a, b) for a, b in zip(mine, others)],
                [jnp.where(own_first, b, a) for a, b in zip(mine, others)],
            )

        column(8 * core, rates_of(rates, 24 * core), outside, (beyond_wide, above, below))
        column(8 - 8 * core, rates_of(rates, 8 + 8 * core), inside, None)
        for t in range(TILES):
            z = march.tile(t)
            even, odd = [], []
            for k in range(4):
                top, bottom = levels[k, t, pl.ds(0, 8)], levels[k, t, pl.ds(8, 8)]
                even.append(jnp.where(low, top, pltpu.roll(bottom, LANES // 2, 1)))
                odd.append(jnp.where(low, pltpu.roll(top, LANES // 2, 1), bottom))
            for k in range(2):
                codes[2 * z, k] = jnp.concatenate(even[2 * k : 2 * k + 2], 0).astype(jnp.int16)
                codes[2 * z + 1, k] = jnp.concatenate(odd[2 * k : 2 * k + 2], 0).astype(jnp.int16)
        return carry

    lax.fori_loop(0, tiles // TILES, work, 0)


def fold_kernel(codes, view, out):
    bricks = codes.shape[0]
    column = side_column(view)
    low = lax.broadcasted_iota(jnp.int32, (8, LANES), 1) < LANES // 2
    for core in range(2):
        base = 16 * core
        side = jnp.where(low, column[base : base + 8], column[base + 8 : base + 16])
        backward = side > 0
        path = jnp.zeros((8, LANES), F32)
        color = [jnp.zeros((8, LANES), F32) for _ in range(3)]
        for k in range(core, bricks, 2):
            values = [decode(codes[k, 0]), decode(codes[k, 1])]
            farther = path + values[1][8:]
            reach = jnp.exp2(side * jnp.where(backward, farther, path))
            path = farther
            color[0] = color[0] + reach * values[0][:8]
            color[1] = color[1] + reach * values[0][8:]
            color[2] = color[2] + reach * values[1][:8]
        passing = jnp.exp2(-path)
        factor = jnp.where(backward, passing, 1.0)
        parts = [c * factor for c in color] + [1.0 - passing]
        for q in range(4):
            out[q, pl.ds(base, 8), :] = parts[q][:, : LANES // 2]
            out[q, pl.ds(base + 8, 8), :] = parts[q][:, LANES // 2 :]


def body(volume, view_side):
    layers, rows, depth = volume.shape
    size_x, size_y = lax.axis_size("bx"), lax.axis_size("by")
    half = rows // 2
    mates = [(i, i ^ 1) for i in range(size_x)]
    chips = [(i, i + 1) for i in range(1, size_x - 1, 2)]
    chips += [(j, i) for i, j in chips]
    across = []
    for i in range(0, size_x, 2):
        for j in range(size_y - 1):
            upper, lower = (i + 1) * size_y + j, i * size_y + j + 1
            across += [(upper, lower), (lower, upper)]
    view = view_side[None, :]
    in_vmem = pl.BlockSpec(memory_space=pltpu.VMEM)
    shape = jax.ShapeDtypeStruct

    def call(kernel, operands, out_shape, scratch, name, cost=0, limit=24, aliases={}):
        return pl.pallas_call(
            kernel,
            out_shape=out_shape,
            in_specs=[in_vmem] * len(operands),
            out_specs=jax.tree.map(lambda _: in_vmem, out_shape),
            scratch_shapes=scratch,
            input_output_aliases=aliases,
            compiler_params=pltpu.CompilerParams(vmem_limit_bytes=limit << 20),
            cost_estimate=pl.CostEstimate(flops=cost, bytes_accessed=2 * layers * rows * depth, transcendentals=0) if cost else None,
            name=name,
        )(*operands)

    work = 40 * layers * half * depth
    face, part = shape((half, depth), BF16), shape((5, 8, depth), F32)
    brick = shape((2 * layers, depth // LANES + 2, half + 16, LANES), F32)
    send, end = call(
        share_kernel, (volume,), (shape((layers + 1, half, depth), BF16), shape((rows, depth), BF16)), [], "share"
    )
    end_in = lax.ppermute(end, "bx", chips)
    mate = lax.ppermute(send, "bx", mates)
    own, field, rates, own_rim = call(
        functools.partial(own_kernel, layers * size_x),
        (volume, view),
        (part, brick, shape((2, rows, LANES), F32), face),
        [],
        "own",
        work // 2,
    )
    rim = call(rim_rows_kernel, (mate, own_rim), shape((2 * layers, depth), BF16), [], "rim_rows")
    beyond = lax.ppermute(rim, ("bx", "by"), across)
    hand_on = call(hand_kernel, (end_in, rim), face, [], "hand")
    handed = lax.ppermute(hand_on, "bx", mates)
    other, field = call(mate_kernel, (mate, rates, field), (part, brick), [], "mate", work // 2, aliases={2: 1})
    wide, rim_wide = pltpu.VMEM((half, depth), F32), pltpu.VMEM((2 * layers, depth), F32)
    border = call(rim_kernel, (beyond, rates, field), part, [rim_wide], "rim", work)
    codes = call(
        outer_kernel,
        (end_in, handed, beyond, rates, own, other, border, field),
        shape((size_x, 2, 16, LANES), jnp.int16),
        [wide, wide, rim_wide, pltpu.VMEM((4, TILES, 16, LANES), jnp.int32)],
        "outer",
        work,
    )
    codes = lax.all_to_all(codes, "bx", split_axis=0, concat_axis=0, tiled=True)
    return call(fold_kernel, (codes, view), shape((4, rows, depth // size_x), F32), [], "fold")


def solution(mesh):
    placed = (P("bx", "by", None), P("by"))
    return jax.shard_map(body, mesh=mesh, in_specs=placed, out_specs=P(None, "by", "bx"), check_vma=False)
```
